256 devices in a mesh: dp: 4 (over x), ctx: 32 (over y, z), head: 2 (over core).
Axes of the slice: x: 4, y: 4, z: 8, core: 2. Of those that a mesh axis runs over, the one named last changes fastest.
Arguments:
- queries: bfloat16 [16384, 32, 128], P(('dp', 'ctx'), 'head'), parts along dimension 0, may hold values from -15 to 15
- key_rows: bfloat16 [16384, 4, 128], P(('dp', 'ctx'), 'head'), parts along dimension 0, may hold values from -15 to 15
- values: bfloat16 [16384, 4, 128], P(('dp', 'ctx'), 'head'), parts along dimension 0, may hold values from -12 to 12
- out_grad: bfloat16 [16384, 32, 128], P(('dp', 'ctx'), 'head'), parts along dimension 0, may hold values from -6 to 6
- doc_lengths: int32 [64], P('dp'), parts along dimension 0, may hold values from 1 to 3072, 4096 in all
Outputs:
- attended: bfloat16 [16384, 32, 128], P(('dp', 'ctx'), 'head'), parts along dimension 0
- query_grad: bfloat16 [16384, 32, 128], P(('dp', 'ctx'), 'head'), parts along dimension 0
- key_grad: bfloat16 [16384, 4, 128], P(('dp', 'ctx'), 'head'), parts along dimension 0
- value_grad: bfloat16 [16384, 4, 128], P(('dp', 'ctx'), 'head'), parts along dimension 0
The draws below stay inside these ranges and needn't reach their ends.
There are 4 independent parts, one for each index of `dp`. The reference program is written for one: setup_inputs(seed, part) draws one part's arguments, and reference() takes and returns one part's arrays. A program takes and returns all parts, laid end to end along the dimension named above; each array names one. Nothing has to cross between parts.
Inputs may be any that keep to these rules, and one draw needn't show every extreme that they name: `doc_lengths`: the lengths sum to 4096; the longest is exactly 3072.
All inputs are finite; a program needn't handle non-finite values.
Results may differ from the reference program's by a relative error of at most 0.03.
Values may be sent and summed in bfloat16 or wider, within the bound.
No kernel may reach another device: no remote copies, remote signals or barrier semaphores. Data moves between devices by JAX's collectives and lax.ppermute only.
A program may use at most 128 MiB of HBM per device.

```python
import math
import jax
import jax.numpy as jnp
import numpy as np
from jax import lax

HEADDIM = 128
QHEADS = 32
KVHEADS = 4
DOCS = 16
SEQ = 4096
MOSTDOC = 3072


def shared_vectors(key):
    return 1.2 * jnp.clip(jax.random.normal(key, (SEQ, KVHEADS, HEADDIM), jnp.float32), -2.5, 2.5)


def draw_key_rows(key, part):
    shared = shared_vectors(key)
    result = shared
    return result.astype(jnp.bfloat16)


def draw_queries(key, part):
    key = jax.random.fold_in(key, 23)
    result = 1.2 * jnp.clip(jax.random.normal(key, (SEQ, QHEADS, HEADDIM), jnp.float32), -5.0, 5.0)
    return result.astype(jnp.bfloat16)


def steps_of(rng, dims, split, low, top_value):
    loudness, own = 1.0, jax.random.fold_in(rng, 6)
    for position, blocks in split:
        steps = jnp.exp(jax.random.uniform(jax.random.fold_in(own, position), (blocks,), jnp.float32, low / len(split), top_value / len(split)))
        loudness = loudness * jnp.repeat(steps, dims[position] // blocks).reshape([-1 if axis == position else 1 for axis in range(len(dims))])
    return loudness


def profile(count, total, limit, skew):
    loads = [(1 << 20) // math.isqrt(rank ** skew) + 1 for rank in range(2, count + 1)]
    rest, holding = total - limit - (count - 1), [1] * (count - 1)
    while rest > 0:
        free = [i for i in range(count - 1) if holding[i] < limit]
        whole, left = sum([loads[i] for i in free]), rest
        for i in free:
            addition = min(limit - holding[i], max(1, left * loads[i] // whole), rest)
            holding[i] = holding[i] + addition
            rest = rest - addition
    return np.array([limit] + holding)


def ragged_sizes(key, count, total, reach, lean):
    if count == 2:
        one = jax.random.randint(key, (), max(1, total - reach), min(reach, total - 1) + 1)
        return jnp.stack([one, total - one])
    lengths = jnp.asarray(profile(count, total, reach, lean), jnp.int32)
    twos = (count - 1) // 2
    source_of, receiver = lengths[1:1 + 2 * twos:2], lengths[2:2 + 2 * twos:2]
    room = jnp.minimum(source_of - 1, reach - receiver)
    moved = jax.random.randint(jax.random.fold_in(key, 1), (twos,), 0, 1 << 20) % (room + 1)
    lengths = lengths.at[1:1 + 2 * twos:2].set(source_of - moved).at[2:2 + 2 * twos:2].set(receiver + moved)
    return lengths[jax.random.permutation(jax.random.fold_in(key, 2), count)]


def bell_draw(rng, extent, width, reach, shards=(), held_as=jnp.bfloat16):
    values = width * jax.random.normal(rng, extent, jnp.float32)
    if shards:
        values = values * steps_of(rng, extent, shards, -0.22, 0.18)
    return jnp.clip(values, -reach, reach).astype(held_as)


def setup_inputs(seed: int = 0, part: int = 0) -> dict:
    streams_of = jax.random.split(jax.random.key(seed), 6)
    part_splits = jax.random.split(jax.random.fold_in(streams_of[5], part), 6)
    return {
        "queries": draw_queries(jax.random.fold_in(jax.random.fold_in(streams_of[5], part), 71), part),
        "key_rows": draw_key_rows(jax.random.fold_in(jax.random.fold_in(streams_of[5], part), 71), part),
        "values": bell_draw(part_splits[2], (SEQ, KVHEADS, HEADDIM), 2.0, 12.0, ((0, 32), (1, 2))),
        "out_grad": bell_draw(part_splits[3], (SEQ, QHEADS, HEADDIM), 1.0, 6.0, ((0, 32), (1, 2))),
        "doc_lengths": ragged_sizes(part_splits[4], DOCS, SEQ, MOSTDOC, 2).astype(jnp.int32),
    }


MASKED_SCORE = -1e+30

def doc_index(positions, bounds):
    return lax.optimization_barrier(jnp.sum((positions[:, None] >= bounds[None, :]).astype(jnp.int32), axis=1))

def rounded(values_f32):
    return lax.optimization_barrier(values_f32.astype(jnp.bfloat16)).astype(jnp.float32)

def reference(queries, key_rows, values, out_grad, doc_lengths):
    seq_len, query_heads, head_size = queries.shape
    key_heads = key_rows.shape[1]
    group_size = query_heads // key_heads
    score_scale = 1.0 / math.sqrt(head_size)
    bounds = jnp.cumsum(doc_lengths).astype(jnp.int32)
    positions = jnp.arange(seq_len, dtype=jnp.int32)
    documents = doc_index(positions, bounds)
    block_rows = math.gcd(128, seq_len)
    keys_f32 = key_rows.astype(jnp.float32)
    values_f32 = values.astype(jnp.float32)

    def one_block(state_now, block_number):
        key_sum, value_sum = state_now
        block_start = (block_number * block_rows).astype(jnp.int32)
        query_block = lax.dynamic_slice_in_dim(queries, block_start, block_rows, 0).astype(jnp.float32)
        query_block = query_block.reshape(block_rows, key_heads, group_size, head_size)
        grad_block = lax.dynamic_slice_in_dim(out_grad, block_start, block_rows, 0).astype(jnp.float32)
        grad_block = grad_block.reshape(block_rows, key_heads, group_size, head_size)
        query_pos = lax.dynamic_slice_in_dim(positions, block_start, block_rows, 0)
        query_doc = lax.dynamic_slice_in_dim(documents, block_start, block_rows, 0)
        allowed = (positions[None, :] <= query_pos[:, None]) & (documents[None, :] == query_doc[:, None])
        allowed = allowed[None, None]
        scores = jnp.einsum('qagd,kad->agqk', query_block, keys_f32) * score_scale
        scores = jnp.where(allowed, scores, MASKED_SCORE)
        row_max = lax.optimization_barrier(jnp.max(scores, axis=-1))
        exp_terms = jnp.where(allowed, jnp.exp(scores - row_max[..., None]), 0.0)
        row_total = lax.optimization_barrier(jnp.sum(exp_terms, axis=-1))
        weighted = jnp.einsum('agqk,kad->agqd', rounded(exp_terms), values_f32)
        attended = rounded(weighted / row_total[..., None])
        log_total = row_max + jnp.log(row_total)
        grad_turned = jnp.transpose(grad_block, (1, 2, 0, 3))
        out_dot = lax.optimization_barrier(jnp.sum(grad_turned * attended, axis=-1))
        probs = jnp.where(allowed, jnp.exp(scores - log_total[..., None]), 0.0)
        dprobs = jnp.einsum('agqd,kad->agqk', grad_turned, values_f32)
        dscores = rounded(probs * (dprobs - out_dot[..., None]))
        query_part = jnp.einsum('agqk,kad->qagd', dscores, keys_f32) * score_scale
        key_sum = key_sum + jnp.einsum('agqk,qagd->kad', dscores, query_block) * score_scale
        value_sum = value_sum + jnp.einsum('agqk,qagd->kad', rounded(probs), grad_block)
        out_rows = jnp.transpose(attended, (2, 0, 1, 3)).reshape(block_rows, query_heads, head_size)
        query_rows = query_part.reshape(block_rows, query_heads, head_size)
        return ((key_sum, value_sum), (out_rows.astype(jnp.bfloat16), query_rows.astype(jnp.bfloat16)))
    empty = jnp.zeros((seq_len, key_heads, head_size), jnp.float32)
    sums, blocks = lax.scan(one_block, (empty, empty), jnp.arange(seq_len // block_rows, dtype=jnp.int32))
    attended = blocks[0].reshape(seq_len, query_heads, head_size)
    query_grad = blocks[1].reshape(seq_len, query_heads, head_size)
    return (attended, query_grad, sums[0].astype(jnp.bfloat16), sums[1].astype(jnp.bfloat16))
```

```python
import functools
import math

import jax
import jax.numpy as jnp
from jax import lax
from jax.experimental import pallas as pl
from jax.experimental.pallas import tpu as pltpu
from jax.sharding import PartitionSpec as P

MASKED_SCORE = -1e30
NY, NZ = 4, 8


def dot_tn(left, right):
    return lax.dot_general(left, right, (((0,), (0,)), ((), ())), preferred_element_type=jnp.float32)


def dot_nt(left, right, precision=None):
    return lax.dot_general(
        left, right, (((1,), (1,)), ((), ())), precision=precision, preferred_element_type=jnp.float32
    )


def dot_nn(left, right):
    return jnp.dot(left, right, preferred_element_type=jnp.float32)


def stage_kernel(stage, waits, block, group, *refs):
    offset, forward, finish, backward, last = stage
    first = forward and offset == 0
    paired = offset not in (0, 4)
    units = 4 if paired else 2
    lanes = block * group
    refs = list(refs)
    take = lambda count: [refs.pop(0) for _ in range(count)]
    take(waits)
    docs_ref, place_ref = take(2)
    q_in = take(2)
    g_in = take(2) if backward else []
    pieces = take(1 if offset == 0 else 2)
    state_in = take(3) if forward and not first else []
    stats_in = take(2) if backward and not finish else []
    dq_in = take(1) if backward and not finish else []
    state_out = take(3) if forward and not finish else []
    rows_out = take(2) if finish or last else []
    stats_out = take(2) if finish else []
    dq_out = take(1) if backward and not last else []
    grads = take(len(pieces)) if backward else []
    k_scr, v_scr, q_scr, s_scr, m_scr = take(5)
    if finish:
        state_out = take(3)
    if backward:
        g_scr, dk_scr, dv_scr = take(3)
    if last:
        dq_out = take(1)
    stats = stats_out or stats_in

    head_size = q_in[0].shape[1]
    scale = 1.0 / math.sqrt(head_size)
    log2_scale = scale * math.log2(math.e)
    y, z = place_ref[0], place_ref[1]

    def block_of(slot, distance):
        return lax.rem(y + NY - slot, NY) * NZ + lax.rem(z + NZ + distance, NZ)

    def blocks_of(unit):
        if paired:
            return block_of(unit, -offset), block_of(unit, offset)
        return block_of(2 * unit, offset), block_of(2 * unit + 1, offset)

    def places():
        for unit in range(units):
            for half in range(2):
                if paired:
                    yield unit, half, half, unit
                else:
                    yield unit, half, unit if offset else 0, half if offset else 2 * unit + half

    for unit, half, piece, slot in places():
        rows = pl.ds(half * block, block)
        k_scr[unit, rows, :] = pieces[piece][slot, 0]
        v_scr[unit, rows, :] = pieces[piece][slot, 1]
    for part in range(2):
        q_scr[part] = q_in[part][...]
        if backward:
            g_scr[part] = g_in[part][...]

    def doc_start(position):
        bound, start = jnp.int32(0), jnp.zeros_like(position)
        for number in range(docs_ref.shape[0]):
            bound = bound + docs_ref[number]
            start = jnp.where(bound <= position, bound, start)
        return start

    def fold(value):
        return value.reshape(value.shape[0] // 8, 8, value.shape[1])

    def part_facts(part):
        query_block = jnp.where(part == 0, y, NY - 1 - y) * NZ + z
        first_pos = query_block * block
        lane = lax.broadcasted_iota(jnp.int32, (1, lanes), 1)
        positions = first_pos + lane // group
        return query_block, positions, doc_start(positions), doc_start(first_pos), doc_start(first_pos + block - 1)

    def is_live(unit, facts):
        query_block, _, _, open_first, _ = facts
        one, two = ((n <= query_block) & ((n + 1) * block > open_first) for n in blocks_of(unit))
        return one | two

    def is_clear(unit, facts):
        query_block, _, _, _, open_last = facts
        one, two = ((n < query_block) & (n * block >= open_last) for n in blocks_of(unit))
        return one & two

    def scores_of(unit, part, facts, masked):
        scores = dot_nt(k_scr[unit], q_scr[part])
        if masked:
            _, positions, starts, _, _ = facts
            one, two = blocks_of(unit)
            row = lax.broadcasted_iota(jnp.int32, (2 * block, lanes), 0)
            key_pos = row + jnp.where(row < block, one, two - 1) * block
            scores = jnp.where((key_pos <= positions) & (key_pos >= starts), scores, MASKED_SCORE)
        return scores

    def each_unit(facts, work):
        def step(unit, _):
            live, clear = is_live(unit, facts), is_clear(unit, facts)
            pl.when(live & clear)(lambda: work(unit, False))
            pl.when(live & jnp.logical_not(clear))(lambda: work(unit, True))
            return 0

        lax.fori_loop(0, units, step, 0)

    def forward_part(part, _):
        facts = part_facts(part)
        m_new, l_new, o_new = state_out
        if first:
            m_old = jnp.full((8, lanes), MASKED_SCORE, jnp.float32)
        else:
            m_old = state_in[0][part]
        m_scr[...] = m_old

        def score(unit, masked):
            scores = scores_of(unit, part, facts, masked)
            s_scr[unit] = scores
            m_scr[...] = jnp.maximum(m_scr[...], jnp.max(fold(scores), axis=0))

        each_unit(facts, score)
        top = jnp.max(m_scr[...], axis=0, keepdims=True)
        m_new[part] = jnp.broadcast_to(top, (8, lanes))
        if first:
            l_new[part] = jnp.zeros((8, lanes), jnp.float32)
            o_new[part] = jnp.zeros((head_size, lanes), jnp.float32)
        else:
            fading = jnp.exp2((m_old - top) * log2_scale)
            l_new[part] = state_in[1][part] * fading
            o_new[part] = state_in[2][part] * fading[:1]
        row_max = top * log2_scale

        def weigh(unit, _):
            @pl.when(is_live(unit, facts))
            def _():
                weights = jnp.exp2(s_scr[unit] * log2_scale - row_max)
                l_new[part] += jnp.sum(fold(weights), axis=0)
                o_new[part] += dot_tn(v_scr[unit], weights.astype(jnp.bfloat16))

            return 0

        lax.fori_loop(0, units, weigh, 0)
        if finish:
            row_total = jnp.sum(l_new[part], axis=0, keepdims=True)
            attended = (o_new[part] / row_total).T.astype(jnp.bfloat16)
            products = attended.astype(jnp.float32) * g_scr[part].astype(jnp.float32)
            stats_out[0][part] = jnp.broadcast_to(row_max + jnp.log2(row_total), (8, lanes))
            stats_out[1][part] = dot_nt(jnp.ones((8, head_size), jnp.float32), products, lax.Precision.HIGHEST)
            write_rows(part, attended)
        return 0

    def write_rows(part, rows):
        for number in range(2):

            @pl.when(part == number)
            def _():
                rows_out[number][...] = rows

    def backward_part(part, _):
        facts = part_facts(part)
        log_total, out_dot = stats[0][part][:1], stats[1][part][:1]
        dq_new = dq_out[0]
        dq_new[part] = jnp.zeros((head_size, lanes), jnp.float32) if finish else dq_in[0][part]

        def differentiate(unit, masked):
            probs = jnp.exp2(scores_of(unit, part, facts, masked) * log2_scale - log_total)
            dprobs = dot_nt(v_scr[unit], g_scr[part])
            dscores = (probs * (dprobs - out_dot)).astype(jnp.bfloat16)
            dv_scr[unit] += dot_nn(probs.astype(jnp.bfloat16), g_scr[part])
            dk_scr[unit] += dot_nn(dscores, q_scr[part])
            dq_new[part] += dot_tn(k_scr[unit], dscores)

        each_unit(facts, differentiate)
        if last:
            write_rows(part, (dq_new[part] * scale).T.astype(jnp.bfloat16))
        return 0

    if forward:
        lax.fori_loop(0, 2, forward_part, 0)
    if backward:
        dk_scr[...] = jnp.zeros_like(dk_scr)
        dv_scr[...] = jnp.zeros_like(dv_scr)
        lax.fori_loop(0, 2, backward_part, 0)
        for unit, half, piece, slot in places():
            rows = pl.ds(half * block, block)
            grads[piece][slot, 0] = (dk_scr[unit, rows, :] * scale).astype(jnp.bfloat16)
            grads[piece][slot, 1] = dv_scr[unit, rows, :].astype(jnp.bfloat16)


def run_stage(stage, block, group, facts, q_parts, g_parts, pieces, state=(), stats=(), dq=(), after=()):
    offset, forward, finish, backward, last = stage
    units = 2 if offset in (0, 4) else 4
    lanes, head_size = q_parts[0].shape
    f32 = lambda *shape: jax.ShapeDtypeStruct(shape, jnp.float32)
    low = lambda array: jax.ShapeDtypeStruct(array.shape, jnp.bfloat16)
    state_shapes = [f32(2, 8, lanes), f32(2, 8, lanes), f32(2, head_size, lanes)]
    dq_shape = f32(2, head_size, lanes)
    operands = [*after, *facts, *q_parts, *(g_parts if backward else ()), *pieces, *state, *stats, *dq]
    outs = []
    aliases = {}
    if forward and not finish:
        if state:
            aliases = {len(operands) - 3 + n: n for n in range(3)}
        outs += state_shapes
    if finish or last:
        outs += [low(q) for q in q_parts]
    if finish:
        outs += state_shapes[:2]
    if backward and not last:
        if dq:
            aliases = {len(operands) - 1: len(outs)}
        outs += [dq_shape]
    if backward:
        outs += [low(piece) for piece in pieces]
    scratch = [
        pltpu.VMEM((units, 2 * block, head_size), jnp.bfloat16),
        pltpu.VMEM((units, 2 * block, head_size), jnp.bfloat16),
        pltpu.VMEM((2, lanes, head_size), jnp.bfloat16),
        pltpu.VMEM((units if forward else 1, 2 * block, lanes), jnp.float32),
        pltpu.VMEM((8, lanes), jnp.float32),
    ]
    if finish:
        scratch += [pltpu.VMEM(shape.shape, jnp.float32) for shape in state_shapes]
    if backward:
        scratch += [
            pltpu.VMEM((2, lanes, head_size), jnp.bfloat16),
            pltpu.VMEM((units, 2 * block, head_size), jnp.float32),
            pltpu.VMEM((units, 2 * block, head_size), jnp.float32),
        ]
    if last:
        scratch += [pltpu.VMEM(dq_shape.shape, jnp.float32)]
    smem = pl.BlockSpec(memory_space=pltpu.SMEM)
    vmem = pl.BlockSpec(memory_space=pltpu.VMEM)
    products = 2 * forward + 5 * backward
    return pl.pallas_call(
        functools.partial(stage_kernel, stage, len(after), block, group),
        out_shape=outs,
        in_specs=[pl.BlockSpec(memory_space=pl.ANY)] * len(after) + [smem, smem] + [vmem] * (len(operands) - 2 - len(after)),
        out_specs=[vmem] * len(outs),
        scratch_shapes=scratch,
        input_output_aliases=aliases,
        compiler_params=pltpu.CompilerParams(vmem_limit_bytes=24 * 1024 * 1024),
        cost_estimate=pl.CostEstimate(
            flops=6 * products * 2 * lanes * units * 2 * block * head_size,
            bytes_accessed=4 * 1024 * 1024,
            transcendentals=2 * lanes * units * 2 * block,
        ),
        name="fwd" * forward + "bwd" * backward + str(offset),
    )(*operands)


def y_turn(turn):
    return [(y * NZ + z, ((y + turn) % NY) * NZ + z) for y in range(NY) for z in range(NZ)]


def z_turn(turn):
    return [(y * NZ + z, y * NZ + (z + turn) % NZ) for y in range(NY) for z in range(NZ)]


MIRROR = [(y * NZ + z, (NY - 1 - y) * NZ + z) for y in range(NY) for z in range(NZ)]


def add_up(one, other):
    return (one.astype(jnp.float32) + other.astype(jnp.float32)).astype(jnp.bfloat16)


def move_right(array):
    return lax.ppermute(array, "ctx", z_turn(1))


def move_left(array):
    return lax.ppermute(array, "ctx", z_turn(-1))


def on_device(queries, key_rows, values, out_grad, doc_lengths):
    block, query_heads, head_size = queries.shape
    key_heads = key_rows.shape[1]
    group = query_heads // key_heads
    place = lax.axis_index("ctx")
    y, z = place // NZ, place % NZ
    mine = y // 2

    def head_of(array, number, width):
        picked = jnp.where(number == 0, array[:, :width], array[:, width:])
        return picked.reshape(block * width, head_size)

    def key_pair(number):
        return jnp.stack([head_of(key_rows, number, 1), head_of(values, number, 1)])

    held = [key_pair(mine)]
    for turn in range(1, NY):
        held.append(lax.ppermute(key_pair(((y + turn) % NY) // 2), "ctx", y_turn(turn)))
    column = jnp.stack(held)

    def both_rows(array):
        return [head_of(array, mine, group), lax.ppermute(head_of(array, 1 - mine, group), "ctx", MIRROR)]

    q_parts, g_parts = both_rows(queries), both_rows(out_grad)
    facts = (doc_lengths, jnp.stack([y, z]).astype(jnp.int32))
    run = functools.partial(run_stage, block=block, group=group, facts=facts, q_parts=q_parts, g_parts=g_parts)

    right, left = [column], [column]
    state = ()
    for step in range(4):
        pieces = [column] if step == 0 else [right[step], left[step]]
        if step < 3:
            right.append(move_right(right[step]))
            left.append(move_left(left[step]))
        else:
            right.append(move_right(right[step][:2]))
            left.append(move_left(left[step][2:]))
        state = run((step, True, False, False, False), pieces=pieces, state=state)
    own_out, other_out, log_total, out_dot, dq, from_right, from_left = run(
        (4, True, True, True, False), pieces=[right[4], left[4]], state=state
    )
    stats = (log_total, out_dot)
    other_out = lax.ppermute(other_out, "ctx", MIRROR)
    from_right, from_left = move_right(from_right), move_left(from_left)
    after = ()
    for step in (3, 2, 1):
        dq, behind, ahead = run(
            (step, False, False, True, False), pieces=[right[step], left[step]], stats=stats, dq=(dq,), after=after
        )
        arrived_right, arrived_left = from_right, from_left
        if step == 3:
            from_right = jnp.concatenate([add_up(ahead[:2], from_right), ahead[2:]], axis=0)
            from_left = jnp.concatenate([behind[:2], add_up(behind[2:], from_left)], axis=0)
        else:
            from_right, from_left = add_up(ahead, from_right), add_up(behind, from_left)
        after = (arrived_right, arrived_left)
        from_right, from_left = move_right(from_right), move_left(from_left)
    own_dq, other_dq, grad = run((0, False, False, True, True), pieces=[column], stats=stats, dq=(dq,), after=after)
    other_dq = lax.ppermute(other_dq, "ctx", MIRROR)
    sums = grad.astype(jnp.float32) + from_right.astype(jnp.float32) + from_left.astype(jnp.float32)

    def both_heads(own, other):
        one, two = (r.reshape(block, group, head_size) for r in (own, other))
        return jnp.concatenate([jnp.where(mine == 0, one, two), jnp.where(mine == 0, two, one)], axis=1)

    attended, query_grad = both_heads(own_out, other_out), both_heads(own_dq, other_dq)
    terms = [(mine, sums[0])]
    for turn in range(1, NY):
        arrived = lax.ppermute(sums[turn].astype(jnp.bfloat16), "ctx", y_turn(-turn)).astype(jnp.float32)
        terms.append((((y + turn) % NY) // 2, arrived))
    heads = [sum(jnp.where(number == head, term, 0.0) for number, term in terms) for head in range(2)]
    grads = jnp.stack(heads, axis=2).astype(jnp.bfloat16)
    return attended, query_grad, grads[0], grads[1]


def solution(mesh):
    placed = (
        P(("dp", "ctx"), "head", None),
        P(("dp", "ctx"), "head", None),
        P(("dp", "ctx"), "head", None),
        P(("dp", "ctx"), "head", None),
        P("dp"),
    )
    return jax.shard_map(
        on_device,
        mesh=mesh,
        in_specs=placed,
        out_specs=(
            P(("dp", "ctx"), "head", None),
            P(("dp", "ctx"), "head", None),
            P(("dp", "ctx"), "head", None),
            P(("dp", "ctx"), "head", None),
        ),
        check_vma=False,
    )
```

```python
import functools
import math

import jax
import jax.numpy as jnp
from jax import lax
from jax.experimental import pallas as pl
from jax.experimental.pallas import tpu as pltpu
from jax.sharding import PartitionSpec as P

MASKED_SCORE = -1e30
NY, NZ = 4, 8


def dot_tn(left, right):
    return lax.dot_general(left, right, (((0,), (0,)), ((), ())), preferred_element_type=jnp.float32)


def dot_nt(left, right):
    return lax.dot_general(left, right, (((1,), (1,)), ((), ())), preferred_element_type=jnp.float32)


def dot_nn(left, right):
    return jnp.dot(left, right, preferred_element_type=jnp.float32)


def stage_kernel(stage, waits, passing, block, group, *refs):
    offset, forward, finish, backward, last = stage
    first = forward and offset == 0
    paired = offset not in (0, 4)
    units = 4 if paired else 2
    lanes = block * group
    refs = list(refs)
    take = lambda count: [refs.pop(0) for _ in range(count)]
    take(waits)
    docs_ref, place_ref = take(2)
    q_in = take(2)
    g_in = take(2) if backward else []
    pieces = take(1 if offset == 0 else 2)
    state_in = take(3) if forward and not first else []
    stats_in = take(2) if backward and not finish else []
    dq_in = take(1) if backward and not finish else []
    take(passing)
    state_out = take(3) if forward and not finish else []
    rows_out = take(2) if finish or last else []
    stats_out = take(2) if finish else []
    dq_out = take(1) if backward and not last else []
    grads = take(len(pieces)) if backward else []
    take(passing)
    k_scr, v_scr, q_scr, s_scr, m_scr = take(5)
    if finish:
        state_out = take(3)
    if backward:
        g_scr, dk_scr, dv_scr = take(3)
    if last:
        dq_out = take(1)
    stats = stats_out or stats_in

    head_size = q_in[0].shape[1]
    scale = 1.0 / math.sqrt(head_size)
    log2_scale = scale * math.log2(math.e)
    y, z = place_ref[0], place_ref[1]

    def block_of(slot, distance):
        return (y ^ slot) * NZ + lax.rem(z + NZ + distance, NZ)

    def blocks_of(unit):
        if paired:
            ahead = jnp.where(lax.rem(z, 2) == 0, offset, -offset)
            return block_of(unit, ahead), block_of(unit, -ahead)
        return block_of(2 * unit, offset), block_of(2 * unit + 1, offset)

    def places():
        for unit in range(units):
            for half in range(2):
                if paired:
                    yield unit, half, half, unit
                else:
                    yield unit, half, unit if offset else 0, half if offset else 2 * unit + half

    for unit, half, piece, slot in places():
        rows = pl.ds(half * block, block)
        k_scr[unit, rows, :] = pieces[piece][slot, 0]
        v_scr[unit, rows, :] = pieces[piece][slot, 1]
    for part in range(2):
        q_scr[part] = q_in[part][...]
        if backward:
            g_scr[part] = g_in[part][...]

    def doc_start(position):
        bound, start = jnp.int32(0), jnp.zeros_like(position)
        for number in range(docs_ref.shape[0]):
            bound = bound + docs_ref[number]
            start = jnp.where(bound <= position, bound, start)
        return start

    def fold(value):
        return value.reshape(value.shape[0] // 8, 8, value.shape[1])

    def part_facts(part):
        query_block = jnp.where(part == 0, y, NY - 1 - y) * NZ + z
        first_pos = query_block * block
        return query_block, doc_start(first_pos), doc_start(first_pos + block - 1)

    def is_live(unit, facts):
        query_block, open_first, _ = facts
        return [(n <= query_block) & ((n + 1) * block > open_first) for n in blocks_of(unit)]

    def is_clear(unit, facts):
        query_block, _, open_last = facts
        one, two = ((n < query_block) & (n * block >= open_last) for n in blocks_of(unit))
        return one & two

    def scores_of(unit, rows, part, facts, masked):
        scores = dot_nt(k_scr[unit, rows, :], q_scr[part])
        if masked:
            lane = lax.broadcasted_iota(jnp.int32, (1, lanes), 1)
            positions = facts[0] * block + lane // group
            one, two = blocks_of(unit)
            row = lax.broadcasted_iota(jnp.int32, scores.shape, 0)
            if scores.shape[0] == block:
                key_pos = row + jnp.where(rows.start == 0, one, two) * block
            else:
                key_pos = row + jnp.where(row < block, one, two - 1) * block
            allowed = (key_pos <= positions) & (key_pos >= doc_start(positions))
            scores = jnp.where(allowed, scores, MASKED_SCORE)
        return scores

    def each_unit(facts, work, masks=True):
        def step(unit, _):
            one, two = is_live(unit, facts)
            both, whole = one & two, pl.ds(0, 2 * block)
            if masks:
                clear = is_clear(unit, facts)
                pl.when(both & clear)(lambda: work(unit, whole, False))
                pl.when(both & jnp.logical_not(clear))(lambda: work(unit, whole, True))
            else:
                pl.when(both)(lambda: work(unit, whole, False))
            half = pl.ds(pl.multiple_of(jnp.where(one, 0, block), block), block)
            pl.when(one ^ two)(lambda: work(unit, half, masks))
            return 0

        lax.fori_loop(0, units, step, 0)

    def forward_part(part, _):
        facts = part_facts(part)
        m_new, l_new, o_new = state_out
        if first:
            m_old = jnp.full((8, lanes), MASKED_SCORE, jnp.float32)
        else:
            m_old = state_in[0][part]
        m_scr[...] = m_old

        def score(unit, rows, masked):
            scores = scores_of(unit, rows, part, facts, masked)
            s_scr[unit, rows, :] = scores
            m_scr[...] = jnp.maximum(m_scr[...], jnp.max(fold(scores), axis=0))

        each_unit(facts, score)
        top = jnp.max(m_scr[...], axis=0, keepdims=True)
        m_new[part] = jnp.broadcast_to(top, (8, lanes))
        if first:
            l_new[part] = jnp.zeros((8, lanes), jnp.float32)
            o_new[part] = jnp.zeros((head_size, lanes), jnp.float32)
        else:
            fading = jnp.exp2((m_old - top) * log2_scale)
            l_new[part] = state_in[1][part] * fading
            o_new[part] = state_in[2][part] * fading[:1]
        row_max = top * log2_scale

        def weigh(unit, rows, _):
            weights = jnp.exp2(s_scr[unit, rows, :] * log2_scale - row_max)
            l_new[part] += jnp.sum(fold(weights), axis=0)
            o_new[part] += dot_tn(v_scr[unit, rows, :], weights.astype(jnp.bfloat16))

        each_unit(facts, weigh, masks=False)
        if finish:
            row_total = jnp.sum(l_new[part], axis=0, keepdims=True)
            attended = (o_new[part] / row_total).T.astype(jnp.bfloat16)
            products = attended.astype(jnp.float32) * g_scr[part].astype(jnp.float32)
            stats_out[0][part] = jnp.broadcast_to(row_max + jnp.log2(row_total), (8, lanes))
            upper = products.astype(jnp.bfloat16)
            lower = (products - upper.astype(jnp.float32)).astype(jnp.bfloat16)
            ones = jnp.ones((8, head_size), jnp.bfloat16)
            stats_out[1][part] = dot_nt(ones, upper) + dot_nt(ones, lower)
            write_rows(part, attended)
        return 0

    def write_rows(part, rows):
        for number in range(2):

            @pl.when(part == number)
            def _():
                rows_out[number][...] = rows

    def backward_part(part, _):
        facts = part_facts(part)
        log_total, out_dot = stats[0][part][:1], stats[1][part][:1]
        dq_new = dq_out[0]
        dq_new[part] = jnp.zeros((head_size, lanes), jnp.float32) if finish else dq_in[0][part]

        def differentiate(unit, rows, masked):
            probs = jnp.exp2(scores_of(unit, rows, part, facts, masked) * log2_scale - log_total)
            dprobs = dot_nt(v_scr[unit, rows, :], g_scr[part])
            dscores = (probs * (dprobs - out_dot)).astype(jnp.bfloat16)
            dv_scr[unit, rows, :] += dot_nn(probs.astype(jnp.bfloat16), g_scr[part])
            dk_scr[unit, rows, :] += dot_nn(dscores, q_scr[part])
            dq_new[part] += dot_tn(k_scr[unit, rows, :], dscores)

        each_unit(facts, differentiate)
        if last:
            write_rows(part, (dq_new[part] * scale).T.astype(jnp.bfloat16))
        return 0

    if forward:
        lax.fori_loop(0, 2, forward_part, 0)
    if backward:
        dk_scr[...] = jnp.zeros_like(dk_scr)
        dv_scr[...] = jnp.zeros_like(dv_scr)
        lax.fori_loop(0, 2, backward_part, 0)
        for unit, half, piece, slot in places():
            rows = pl.ds(half * block, block)
            grads[piece][slot, 0] = (dk_scr[unit, rows, :] * scale).astype(jnp.bfloat16)
            grads[piece][slot, 1] = dv_scr[unit, rows, :].astype(jnp.bfloat16)


def run_stage(stage, block, group, facts, q_parts, g_parts, pieces, state=(), stats=(), dq=(), after=(), passing=()):
    offset, forward, finish, backward, last = stage
    units = 2 if offset in (0, 4) else 4
    lanes, head_size = q_parts[0].shape
    f32 = lambda *shape: jax.ShapeDtypeStruct(shape, jnp.float32)
    low = lambda array: jax.ShapeDtypeStruct(array.shape, jnp.bfloat16)
    state_shapes = [f32(2, 8, lanes), f32(2, 8, lanes), f32(2, head_size, lanes)]
    dq_shape = f32(2, head_size, lanes)
    operands = [*after, *facts, *q_parts, *(g_parts if backward else ()), *pieces, *state, *stats, *dq, *passing]
    outs = []
    aliases = {}
    if forward and not finish:
        if state:
            aliases = {len(operands) - 3 + n: n for n in range(3)}
        outs += state_shapes
    if finish or last:
        outs += [low(q) for q in q_parts]
    if finish:
        outs += state_shapes[:2]
    if backward and not last:
        if dq:
            aliases = {len(operands) - 1: len(outs)}
        outs += [dq_shape]
    if backward:
        outs += [low(piece) for piece in pieces]
    for number, array in enumerate(passing):
        aliases[len(operands) - len(passing) + number] = len(outs)
        outs += [low(array)]
    scratch = [
        pltpu.VMEM((units, 2 * block, head_size), jnp.bfloat16),
        pltpu.VMEM((units, 2 * block, head_size), jnp.bfloat16),
        pltpu.VMEM((2, lanes, head_size), jnp.bfloat16),
        pltpu.VMEM((units if forward else 1, 2 * block, lanes), jnp.float32),
        pltpu.VMEM((8, lanes), jnp.float32),
    ]
    if finish:
        scratch += [pltpu.VMEM(shape.shape, jnp.float32) for shape in state_shapes]
    if backward:
        scratch += [
            pltpu.VMEM((2, lanes, head_size), jnp.bfloat16),
            pltpu.VMEM((units, 2 * block, head_size), jnp.float32),
            pltpu.VMEM((units, 2 * block, head_size), jnp.float32),
        ]
    if last:
        scratch += [pltpu.VMEM(dq_shape.shape, jnp.float32)]
    smem = pl.BlockSpec(memory_space=pltpu.SMEM)
    vmem = pl.BlockSpec(memory_space=pltpu.VMEM)
    anywhere = pl.BlockSpec(memory_space=pl.ANY)
    inside = len(operands) - 2 - len(after) - len(passing)
    products = 2 * forward + 5 * backward
    return pl.pallas_call(
        functools.partial(stage_kernel, stage, len(after), len(passing), block, group),
        out_shape=outs,
        in_specs=[anywhere] * len(after) + [smem, smem] + [vmem] * inside + [anywhere] * len(passing),
        out_specs=[vmem] * (len(outs) - len(passing)) + [anywhere] * len(passing),
        scratch_shapes=scratch,
        input_output_aliases=aliases,
        compiler_params=pltpu.CompilerParams(vmem_limit_bytes=24 * 1024 * 1024),
        cost_estimate=pl.CostEstimate(
            flops=6 * products * 2 * lanes * units * 2 * block * head_size,
            bytes_accessed=4 * 1024 * 1024,
            transcendentals=2 * lanes * units * 2 * block,
        ),
        name="fwd" * forward + "bwd" * backward + str(offset),
    )(*operands)


def swap_y(mask):
    return [(y * NZ + z, (y ^ mask) * NZ + z) for y in range(NY) for z in range(NZ)]


def swap_z(first):
    turns = [1 if z % 2 == first else -1 for z in range(NZ)]
    return [(y * NZ + z, y * NZ + (z + turns[z]) % NZ) for y in range(NY) for z in range(NZ)]


MIRROR = swap_y(NY - 1)


def add_up(one, other):
    return (one.astype(jnp.float32) + other.astype(jnp.float32)).astype(jnp.bfloat16)


def swap_even(array):
    return lax.ppermute(array, "ctx", swap_z(0))


def swap_odd(array):
    return lax.ppermute(array, "ctx", swap_z(1))


def on_device(queries, key_rows, values, out_grad, doc_lengths):
    block, query_heads, head_size = queries.shape
    key_heads = key_rows.shape[1]
    group = query_heads // key_heads
    place = lax.axis_index("ctx")
    y, z = place // NZ, place % NZ
    mine = y // 2

    def head_of(array, number, width):
        picked = jnp.where(number == 0, array[:, :width], array[:, width:])
        return picked.reshape(block * width, head_size)

    def key_pair(number):
        return jnp.stack([head_of(key_rows, number, 1), head_of(values, number, 1)])

    pairs = [key_pair(mine), key_pair(1 - mine)]
    held = {mask: lax.ppermute(pairs[mask // 2], "ctx", swap_y(mask)) for mask in (1, 3, 2)}
    column = jnp.stack([pairs[0], held[1], held[2], held[3]])

    q_parts = [head_of(queries, mine, group), lax.ppermute(head_of(queries, 1 - mine, group), "ctx", MIRROR)]
    g_own, g_leaving = head_of(out_grad, mine, group), head_of(out_grad, 1 - mine, group)
    facts = (doc_lengths, jnp.stack([y, z]).astype(jnp.int32))
    run = functools.partial(run_stage, block=block, group=group, facts=facts, q_parts=q_parts)

    evens, odds = [column], [column]
    state = ()
    for step in range(4):
        pieces = [column] if step == 0 else [evens[step], odds[step]]
        if step < 3:
            even, odd = swap_even(odds[step]), swap_odd(evens[step])
        else:
            even, odd = swap_even(odds[step][:2]), swap_odd(evens[step][2:])
        evens.append(even)
        odds.append(odd)
        passing = () if step else (g_leaving,)
        state = run((step, True, False, False, False), g_parts=(), pieces=pieces, state=state, passing=passing)
        if passing:
            g_parts = [g_own, lax.ppermute(state[3], "ctx", MIRROR)]
            state = state[:3]
    run = functools.partial(run, g_parts=g_parts)
    own_out, other_out, log_total, out_dot, dq, even_grad, odd_grad = run(
        (4, True, True, True, False), pieces=[evens[4], odds[4]], state=state
    )
    stats = (log_total, out_dot)
    other_out = lax.ppermute(other_out, "ctx", MIRROR)
    even, odd = swap_even(even_grad), swap_odd(odd_grad)
    after = ()
    for step in (3, 2, 1):
        dq, even_grad, odd_grad = run(
            (step, False, False, True, False), pieces=[evens[step], odds[step]], stats=stats, dq=(dq,), after=after
        )
        if step == 3:
            odd_grad = jnp.concatenate([add_up(odd_grad[:2], even), odd_grad[2:]], axis=0)
            even_grad = jnp.concatenate([even_grad[:2], add_up(even_grad[2:], odd)], axis=0)
        else:
            odd_grad, even_grad = add_up(odd_grad, even), add_up(even_grad, odd)
        after = (even, odd)
        even, odd = swap_even(even_grad), swap_odd(odd_grad)
    own_dq, other_dq, grad = run((0, False, False, True, True), pieces=[column], stats=stats, dq=(dq,), after=after)
    other_dq = lax.ppermute(other_dq, "ctx", MIRROR)
    sums = grad.astype(jnp.float32) + even.astype(jnp.float32) + odd.astype(jnp.float32)

    def both_heads(own, other):
        one, two = (r.reshape(block, group, head_size) for r in (own, other))
        return jnp.concatenate([jnp.where(mine == 0, one, two), jnp.where(mine == 0, two, one)], axis=1)

    attended, query_grad = both_heads(own_out, other_out), both_heads(own_dq, other_dq)
    arrived = {
        mask: lax.ppermute(sums[mask].astype(jnp.bfloat16), "ctx", swap_y(mask)).astype(jnp.float32)
        for mask in (1, 3, 2)
    }
    near, far = sums[0] + arrived[1], arrived[2] + arrived[3]
    heads = [jnp.where(mine == 0, near, far), jnp.where(mine == 0, far, near)]
    grads = jnp.stack(heads, axis=2).astype(jnp.bfloat16)
    return attended, query_grad, grads[0], grads[1]


def solution(mesh):
    placed = (
        P(("dp", "ctx"), "head", None),
        P(("dp", "ctx"), "head", None),
        P(("dp", "ctx"), "head", None),
        P(("dp", "ctx"), "head", None),
        P("dp"),
    )
    return jax.shard_map(
        on_device,
        mesh=mesh,
        in_specs=placed,
        out_specs=(
            P(("dp", "ctx"), "head", None),
            P(("dp", "ctx"), "head", None),
            P(("dp", "ctx"), "head", None),
            P(("dp", "ctx"), "head", None),
        ),
        check_vma=False,
    )
```

```python
import functools
import math

import jax
import jax.numpy as jnp
from jax import lax
from jax.experimental import pallas as pl
from jax.experimental.pallas import tpu as pltpu
from jax.sharding import PartitionSpec as P

MASKED_SCORE = -1e30
NY, NZ = 4, 8


def dot_tn(left, right):
    return lax.dot_general(left, right, (((0,), (0,)), ((), ())), preferred_element_type=jnp.float32)


def dot_nt(left, right):
    return lax.dot_general(left, right, (((1,), (1,)), ((), ())), preferred_element_type=jnp.float32)


def dot_nn(left, right):
    return jnp.dot(left, right, preferred_element_type=jnp.float32)


def stage_kernel(stage, waits, passing, block, group, *refs):
    offset, forward, finish, backward, last = stage
    first = forward and offset == 0
    paired = offset not in (0, 4)
    units = 4 if paired else 2
    lanes = block * group
    refs = list(refs)
    take = lambda count: [refs.pop(0) for _ in range(count)]
    take(waits)
    docs_ref, place_ref = take(2)
    q_in = take(2)
    g_in = take(2) if backward else []
    pieces = take(1 if offset == 0 else 2)
    state_in = take(3) if forward and not first else []
    stats_in = take(2) if backward and not finish else []
    dq_in = take(1) if backward and not finish else []
    take(passing)
    state_out = take(3) if forward and not finish else []
    rows_out = take(2) if finish or last else []
    stats_out = take(2) if finish else []
    dq_out = take(1) if backward and not last else []
    grads = take(len(pieces)) if backward else []
    take(passing)
    k_scr, v_scr, q_scr = take(3)
    if finish:
        state_out = take(3)
    if backward:
        g_scr, dk_scr, dv_scr = take(3)
    if last:
        dq_out = take(1)
    stats = stats_out or stats_in

    head_size = q_in[0].shape[1]
    scale = 1.0 / math.sqrt(head_size)
    log2_scale = scale * math.log2(math.e)
    y, z = place_ref[0], place_ref[1]

    def block_of(slot, distance):
        return (y ^ slot ^ (slot >> 1)) * NZ + lax.rem(z + NZ + distance, NZ)

    def blocks_of(unit):
        if paired:
            ahead = jnp.where(lax.rem(z, 2) == 0, offset, -offset)
            return block_of(unit, ahead), block_of(unit, -ahead)
        return block_of(2 * unit, offset), block_of(2 * unit + 1, offset)

    def places():
        for unit in range(units):
            for half in range(2):
                if paired:
                    yield unit, half, half, unit
                else:
                    yield unit, half, unit if offset else 0, half if offset else 2 * unit + half

    for unit, half, piece, slot in places():
        rows = pl.ds(half * block, block)
        k_scr[unit, rows, :] = pieces[piece][slot, 0]
        v_scr[unit, rows, :] = pieces[piece][slot, 1]
    for part in range(2):
        q_scr[part] = q_in[part][...]
        if backward:
            g_scr[part] = g_in[part][...]

    def doc_start(position):
        bound, start = jnp.int32(0), jnp.zeros_like(position)
        for number in range(docs_ref.shape[0]):
            bound = bound + docs_ref[number]
            start = jnp.where(bound <= position, bound, start)
        return start

    def fold(value):
        return value.reshape(value.shape[0] // 8, 8, value.shape[1])

    def part_facts(part):
        query_block = jnp.where(part == 0, y, NY - 1 - y) * NZ + z
        first_pos = query_block * block
        return query_block, doc_start(first_pos), doc_start(first_pos + block - 1)

    def is_live(unit, facts):
        query_block, open_first, _ = facts
        return [(n <= query_block) & ((n + 1) * block > open_first) for n in blocks_of(unit)]

    def is_clear(unit, facts):
        query_block, _, open_last = facts
        one, two = ((n < query_block) & (n * block >= open_last) for n in blocks_of(unit))
        return one & two

    def scores_of(unit, rows, part, facts, masked):
        scores = dot_nt(k_scr[unit, rows, :], q_scr[part])
        if masked:
            lane = lax.broadcasted_iota(jnp.int32, (1, lanes), 1)
            positions = facts[0] * block + lane // group
            one, two = blocks_of(unit)
            row = lax.broadcasted_iota(jnp.int32, scores.shape, 0)
            if scores.shape[0] == block:
                key_pos = row + jnp.where(rows.start == 0, one, two) * block
            else:
                key_pos = row + jnp.where(row < block, one, two - 1) * block
            allowed = (key_pos <= positions) & (key_pos >= doc_start(positions))
            scores = jnp.where(allowed, scores, MASKED_SCORE)
        return scores

    def each_unit(facts, work):
        def step(unit, _):
            one, two = is_live(unit, facts)
            both, whole = one & two, pl.ds(0, 2 * block)
            clear = is_clear(unit, facts)
            pl.when(both & clear)(lambda: work(unit, whole, False))
            pl.when(both & jnp.logical_not(clear))(lambda: work(unit, whole, True))
            half = pl.ds(pl.multiple_of(jnp.where(one, 0, block), block), block)
            pl.when(one ^ two)(lambda: work(unit, half, True))
            return 0

        lax.fori_loop(0, units, step, 0)

    def forward_part(part, _):
        facts = part_facts(part)
        m_new, l_new, o_new = state_out
        if first:
            m_new[part] = jnp.full((8, lanes), MASKED_SCORE, jnp.float32)
            l_new[part] = jnp.zeros((8, lanes), jnp.float32)
            o_new[part] = jnp.zeros((head_size, lanes), jnp.float32)
        else:
            for old, new in zip(state_in, state_out):
                new[part] = old[part]

        def attend(unit, rows, masked):
            scores = scores_of(unit, rows, part, facts, masked)
            m_old = m_new[part]
            top = jnp.maximum(m_old, jnp.max(scores, axis=0, keepdims=True))
            fading = jnp.exp2((m_old - top) * log2_scale)
            weights = jnp.exp2(scores * log2_scale - top[:1] * log2_scale)
            m_new[part] = top
            l_new[part] = l_new[part] * fading + jnp.sum(fold(weights), axis=0)
            added = dot_tn(v_scr[unit, rows, :], weights.astype(jnp.bfloat16))
            o_new[part] = o_new[part] * fading[:1] + added

        each_unit(facts, attend)
        row_max = m_new[part][:1] * log2_scale
        if finish:
            row_total = jnp.sum(l_new[part], axis=0, keepdims=True)
            attended = (o_new[part] / row_total).T.astype(jnp.bfloat16)
            products = attended.astype(jnp.float32) * g_scr[part].astype(jnp.float32)
            stats_out[0][part] = jnp.broadcast_to(row_max + jnp.log2(row_total), (8, lanes))
            upper = products.astype(jnp.bfloat16)
            lower = (products - upper.astype(jnp.float32)).astype(jnp.bfloat16)
            ones = jnp.ones((8, head_size), jnp.bfloat16)
            stats_out[1][part] = dot_nt(ones, upper) + dot_nt(ones, lower)
            write_rows(part, attended)
        return 0

    def write_rows(part, rows):
        for number in range(2):

            @pl.when(part == number)
            def _():
                rows_out[number][...] = rows

    def backward_part(part, _):
        facts = part_facts(part)
        log_total, out_dot = stats[0][part][:1], stats[1][part][:1]
        dq_new = dq_out[0]
        dq_new[part] = jnp.zeros((head_size, lanes), jnp.float32) if finish else dq_in[0][part]

        def differentiate(unit, rows, masked):
            probs = jnp.exp2(scores_of(unit, rows, part, facts, masked) * log2_scale - log_total)
            dprobs = dot_nt(v_scr[unit, rows, :], g_scr[part])
            dscores = (probs * (dprobs - out_dot)).astype(jnp.bfloat16)
            dv_scr[unit, rows, :] += dot_nn(probs.astype(jnp.bfloat16), g_scr[part])
            dk_scr[unit, rows, :] += dot_nn(dscores, q_scr[part])
            dq_new[part] += dot_tn(k_scr[unit, rows, :], dscores)

        each_unit(facts, differentiate)
        if last:
            write_rows(part, (dq_new[part] * scale).T.astype(jnp.bfloat16))
        return 0

    if forward:
        lax.fori_loop(0, 2, forward_part, 0)
    if backward:
        dk_scr[...] = jnp.zeros_like(dk_scr)
        dv_scr[...] = jnp.zeros_like(dv_scr)
        lax.fori_loop(0, 2, backward_part, 0)
        for unit, half, piece, slot in places():
            rows = pl.ds(half * block, block)
            grads[piece][slot, 0] = (dk_scr[unit, rows, :] * scale).astype(jnp.bfloat16)
            grads[piece][slot, 1] = dv_scr[unit, rows, :].astype(jnp.bfloat16)


def run_stage(stage, block, group, facts, q_parts, g_parts, pieces, state=(), stats=(), dq=(), after=(), passing=()):
    offset, forward, finish, backward, last = stage
    units = 2 if offset in (0, 4) else 4
    lanes, head_size = q_parts[0].shape
    f32 = lambda *shape: jax.ShapeDtypeStruct(shape, jnp.float32)
    low = lambda array: jax.ShapeDtypeStruct(array.shape, jnp.bfloat16)
    state_shapes = [f32(2, 8, lanes), f32(2, 8, lanes), f32(2, head_size, lanes)]
    dq_shape = f32(2, head_size, lanes)
    operands = [*after, *facts, *q_parts, *(g_parts if backward else ()), *pieces, *state, *stats, *dq, *passing]
    outs = []
    aliases = {}
    if forward and not finish:
        if state:
            aliases = {len(operands) - 3 + n: n for n in range(3)}
        outs += state_shapes
    if finish or last:
        outs += [low(q) for q in q_parts]
    if finish:
        outs += state_shapes[:2]
    if backward and not last:
        if dq:
            aliases = {len(operands) - 1: len(outs)}
        outs += [dq_shape]
    if backward:
        outs += [low(piece) for piece in pieces]
    for number, array in enumerate(passing):
        aliases[len(operands) - len(passing) + number] = len(outs)
        outs += [low(array)]
    scratch = [
        pltpu.VMEM((units, 2 * block, head_size), jnp.bfloat16),
        pltpu.VMEM((units, 2 * block, head_size), jnp.bfloat16),
        pltpu.VMEM((2, lanes, head_size), jnp.bfloat16),
    ]
    if finish:
        scratch += [pltpu.VMEM(shape.shape, jnp.float32) for shape in state_shapes]
    if backward:
        scratch += [
            pltpu.VMEM((2, lanes, head_size), jnp.bfloat16),
            pltpu.VMEM((units, 2 * block, head_size), jnp.float32),
            pltpu.VMEM((units, 2 * block, head_size), jnp.float32),
        ]
    if last:
        scratch += [pltpu.VMEM(dq_shape.shape, jnp.float32)]
    smem = pl.BlockSpec(memory_space=pltpu.SMEM)
    vmem = pl.BlockSpec(memory_space=pltpu.VMEM)
    anywhere = pl.BlockSpec(memory_space=pl.ANY)
    inside = len(operands) - 2 - len(after) - len(passing)
    products = 2 * forward + 5 * backward
    return pl.pallas_call(
        functools.partial(stage_kernel, stage, len(after), len(passing), block, group),
        out_shape=outs,
        in_specs=[anywhere] * len(after) + [smem, smem] + [vmem] * inside + [anywhere] * len(passing),
        out_specs=[vmem] * (len(outs) - len(passing)) + [anywhere] * len(passing),
        scratch_shapes=scratch,
        input_output_aliases=aliases,
        compiler_params=pltpu.CompilerParams(vmem_limit_bytes=24 * 1024 * 1024),
        cost_estimate=pl.CostEstimate(
            flops=6 * products * 2 * lanes * units * 2 * block * head_size,
            bytes_accessed=4 * 1024 * 1024,
            transcendentals=2 * lanes * units * 2 * block,
        ),
        name="fwd" * forward + "bwd" * backward + str(offset),
    )(*operands)


def swap_y(mask):
    return [(y * NZ + z, (y ^ mask) * NZ + z) for y in range(NY) for z in range(NZ)]


def swap_z(first):
    turns = [1 if z % 2 == first else -1 for z in range(NZ)]
    return [(y * NZ + z, y * NZ + (z + turns[z]) % NZ) for y in range(NY) for z in range(NZ)]


MIRROR = swap_y(NY - 1)


def add_up(one, other):
    return (one.astype(jnp.float32) + other.astype(jnp.float32)).astype(jnp.bfloat16)


def swap_even(array):
    return lax.ppermute(array, "ctx", swap_z(0))


def swap_odd(array):
    return lax.ppermute(array, "ctx", swap_z(1))


def on_device(queries, key_rows, values, out_grad, doc_lengths):
    block, query_heads, head_size = queries.shape
    key_heads = key_rows.shape[1]
    group = query_heads // key_heads
    place = lax.axis_index("ctx")
    y, z = place // NZ, place % NZ
    mine = y // 2

    def head_of(array, number, width):
        picked = jnp.where(number == 0, array[:, :width], array[:, width:])
        return picked.reshape(block * width, head_size)

    def key_pair(number):
        return jnp.stack([head_of(key_rows, number, 1), head_of(values, number, 1)])

    held = key_pair(mine)
    mirrored = lax.ppermute(key_pair(1 - mine), "ctx", MIRROR)
    from_mate = lax.ppermute(jnp.stack([held, mirrored]), "ctx", swap_y(1))
    column = jnp.stack([held, from_mate[0], mirrored, from_mate[1]])

    q_parts = [head_of(queries, mine, group), lax.ppermute(head_of(queries, 1 - mine, group), "ctx", MIRROR)]
    g_own, g_leaving = head_of(out_grad, mine, group), head_of(out_grad, 1 - mine, group)
    facts = (doc_lengths, jnp.stack([y, z]).astype(jnp.int32))
    run = functools.partial(run_stage, block=block, group=group, facts=facts, q_parts=q_parts)

    evens, odds = [column], [column]
    state = ()
    for step in range(4):
        pieces = [column] if step == 0 else [evens[step], odds[step]]
        if step < 3:
            even, odd = swap_even(odds[step]), swap_odd(evens[step])
        else:
            even, odd = swap_even(odds[step][:2]), swap_odd(evens[step][2:])
        evens.append(even)
        odds.append(odd)
        passing = () if step else (g_leaving,)
        state = run((step, True, False, False, False), g_parts=(), pieces=pieces, state=state, passing=passing)
        if passing:
            g_parts = [g_own, lax.ppermute(state[3], "ctx", MIRROR)]
            state = state[:3]
    run = functools.partial(run, g_parts=g_parts)
    own_out, other_out, log_total, out_dot, dq, even_grad, odd_grad = run(
        (4, True, True, True, False), pieces=[evens[4], odds[4]], state=state
    )
    stats = (log_total, out_dot)
    other_out = lax.ppermute(other_out, "ctx", MIRROR)
    even, odd = swap_even(even_grad), swap_odd(odd_grad)
    after = ()
    for step in (3, 2, 1):
        dq, even_grad, odd_grad = run(
            (step, False, False, True, False), pieces=[evens[step], odds[step]], stats=stats, dq=(dq,), after=after
        )
        if step == 3:
            odd_grad = jnp.concatenate([add_up(odd_grad[:2], even), odd_grad[2:]], axis=0)
            even_grad = jnp.concatenate([even_grad[:2], add_up(even_grad[2:], odd)], axis=0)
        else:
            odd_grad, even_grad = add_up(odd_grad, even), add_up(even_grad, odd)
        after = (even_grad, odd_grad)
        even, odd = swap_even(even_grad), swap_odd(odd_grad)
    own_dq, other_dq, grad, other_out = run(
        (0, False, False, True, True), pieces=[column], stats=stats, dq=(dq,), after=after, passing=(other_out,)
    )
    other_dq = lax.ppermute(other_dq, "ctx", MIRROR)
    sums = grad.astype(jnp.float32) + even.astype(jnp.float32) + odd.astype(jnp.float32)

    def both_heads(own, other):
        one, two = (r.reshape(block, group, head_size) for r in (own, other))
        return jnp.concatenate([jnp.where(mine == 0, one, two), jnp.where(mine == 0, two, one)], axis=1)

    attended, query_grad = both_heads(own_out, other_out), both_heads(own_dq, other_dq)
    arrived = {
        mask: lax.ppermute(sums[slot].astype(jnp.bfloat16), "ctx", swap_y(mask)).astype(jnp.float32)
        for slot, mask in ((3, 2), (2, 3), (1, 1))
    }
    near, far = sums[0] + arrived[1], arrived[2] + arrived[3]
    heads = [jnp.where(mine == 0, near, far), jnp.where(mine == 0, far, near)]
    grads = jnp.stack(heads, axis=2).astype(jnp.bfloat16)
    return attended, query_grad, grads[0], grads[1]


def solution(mesh):
    placed = (
        P(("dp", "ctx"), "head", None),
        P(("dp", "ctx"), "head", None),
        P(("dp", "ctx"), "head", None),
        P(("dp", "ctx"), "head", None),
        P("dp"),
    )
    return jax.shard_map(
        on_device,
        mesh=mesh,
        in_specs=placed,
        out_specs=(
            P(("dp", "ctx"), "head", None),
            P(("dp", "ctx"), "head", None),
            P(("dp", "ctx"), "head", None),
            P(("dp", "ctx"), "head", None),
        ),
        check_vma=False,
    )
```

```python
import functools
import math

import jax
import jax.numpy as jnp
from jax import lax
from jax.experimental import pallas as pl
from jax.experimental.pallas import tpu as pltpu
from jax.sharding import PartitionSpec as P

MASKED_SCORE = -1e30
NY, NZ = 4, 8


def dot_tn(left, right):
    return lax.dot_general(left, right, (((0,), (0,)), ((), ())), preferred_element_type=jnp.float32)


def dot_nt(left, right):
    return lax.dot_general(left, right, (((1,), (1,)), ((), ())), preferred_element_type=jnp.float32)


def dot_nn(left, right):
    return jnp.dot(left, right, preferred_element_type=jnp.float32)


def stage_kernel(stage, waits, passing, block, group, *refs):
    kind, forward, finish, backward, last = stage
    first = forward and kind == "own"
    paired = kind == "pair"
    units = 4 if paired else 2
    lanes = block * group
    refs = list(refs)
    take = lambda count: [refs.pop(0) for _ in range(count)]
    take(waits)
    docs_ref, place_ref = take(2)
    q_in = take(2)
    g_in = take(2) if backward else []
    pieces = take(1 if kind == "own" else 2)
    state_in = take(3) if forward and not first else []
    stats_in = take(2) if backward and not finish else []
    dq_in = take(1) if backward and not finish else []
    take(passing)
    state_out = take(3) if forward and not finish else []
    rows_out = take(2) if finish or last else []
    stats_out = take(2) if finish else []
    dq_out = take(1) if backward and not last else []
    grads = take(len(pieces)) if backward else []
    take(passing)
    k_scr, v_scr, q_scr = take(3)
    if finish:
        state_out = take(3)
    if backward:
        g_scr, dk_scr, dv_scr = take(3)
    if last:
        dq_out = take(1)
    stats = stats_out or stats_in

    head_size = q_in[0].shape[1]
    scale = 1.0 / math.sqrt(head_size)
    log2_scale = scale * math.log2(math.e)
    y, z, distance = place_ref[0], place_ref[1], place_ref[2]

    def block_of(slot, steps):
        return (y ^ slot ^ (slot >> 1)) * NZ + lax.rem(z + NZ + steps, NZ)

    def blocks_of(unit):
        if paired:
            return block_of(unit, distance), block_of(unit, -distance)
        return block_of(2 * unit, distance), block_of(2 * unit + 1, distance)

    def places():
        for unit in range(units):
            for half in range(2):
                if paired:
                    yield unit, half, half, unit
                else:
                    yield (unit, half, 0, 2 * unit + half) if kind == "own" else (unit, half, unit, half)

    for unit, half, piece, slot in places():
        rows = pl.ds(half * block, block)
        k_scr[unit, rows, :] = pieces[piece][slot, 0]
        v_scr[unit, rows, :] = pieces[piece][slot, 1]
    for part in range(2):
        q_scr[part] = q_in[part][...]
        if backward:
            g_scr[part] = g_in[part][...]

    def doc_start(position):
        bound, start = jnp.int32(0), jnp.zeros_like(position)
        for number in range(docs_ref.shape[0]):
            bound = bound + docs_ref[number]
            start = jnp.where(bound <= position, bound, start)
        return start

    def fold(value):
        return value.reshape(value.shape[0] // 8, 8, value.shape[1])

    def part_facts(part):
        query_block = jnp.where(part == 0, y, NY - 1 - y) * NZ + z
        first_pos = query_block * block
        return query_block, doc_start(first_pos), doc_start(first_pos + block - 1)

    def is_live(unit, facts):
        query_block, open_first, _ = facts
        return [(n <= query_block) & ((n + 1) * block > open_first) for n in blocks_of(unit)]

    def is_clear(unit, facts):
        query_block, _, open_last = facts
        one, two = ((n < query_block) & (n * block >= open_last) for n in blocks_of(unit))
        return one & two

    def scores_of(unit, rows, part, facts, masked):
        scores = dot_nt(k_scr[unit, rows, :], q_scr[part])
        if masked:
            lane = lax.broadcasted_iota(jnp.int32, (1, lanes), 1)
            positions = facts[0] * block + lane // group
            one, two = blocks_of(unit)
            row = lax.broadcasted_iota(jnp.int32, scores.shape, 0)
            key_pos = row + jnp.where(rows.start == 0, one, two) * block
            allowed = (key_pos <= positions) & (key_pos >= doc_start(positions))
            scores = jnp.where(allowed, scores, MASKED_SCORE)
        return scores

    def each_unit(facts, work):
        def step(unit, _):
            one, two = is_live(unit, facts)
            clear = is_clear(unit, facts) & one & two
            pl.when(clear)(lambda: work(unit, pl.ds(0, 2 * block), False))

            def half_step(half, _):
                live = jnp.where(half == 0, one, two) & jnp.logical_not(clear)
                rows = pl.ds(pl.multiple_of(half * block, block), block)
                pl.when(live)(lambda: work(unit, rows, True))
                return 0

            lax.fori_loop(0, 2, half_step, 0)
            return 0

        lax.fori_loop(0, units, step, 0)

    def forward_part(part, _):
        facts = part_facts(part)
        m_new, l_new, o_new = state_out
        if first:
            m_new[part] = jnp.full((8, lanes), MASKED_SCORE, jnp.float32)
            l_new[part] = jnp.zeros((8, lanes), jnp.float32)
            o_new[part] = jnp.zeros((head_size, lanes), jnp.float32)
        else:
            for old, new in zip(state_in, state_out):
                new[part] = old[part]

        def attend(unit, rows, masked):
            scores = scores_of(unit, rows, part, facts, masked)
            m_old = m_new[part]
            top = jnp.maximum(m_old, jnp.max(scores, axis=0, keepdims=True))
            fading = jnp.exp2((m_old - top) * log2_scale)
            weights = jnp.exp2(scores * log2_scale - top[:1] * log2_scale)
            m_new[part] = top
            l_new[part] = l_new[part] * fading + jnp.sum(fold(weights), axis=0)
            added = dot_tn(v_scr[unit, rows, :], weights.astype(jnp.bfloat16))
            o_new[part] = o_new[part] * fading[:1] + added

        each_unit(facts, attend)
        row_max = m_new[part][:1] * log2_scale
        if finish:
            row_total = jnp.sum(l_new[part], axis=0, keepdims=True)
            attended = (o_new[part] / row_total).T.astype(jnp.bfloat16)
            products = attended.astype(jnp.float32) * g_scr[part].astype(jnp.float32)
            stats_out[0][part] = jnp.broadcast_to(row_max + jnp.log2(row_total), (8, lanes))
            upper = products.astype(jnp.bfloat16)
            lower = (products - upper.astype(jnp.float32)).astype(jnp.bfloat16)
            ones = jnp.ones((8, head_size), jnp.bfloat16)
            stats_out[1][part] = dot_nt(ones, upper) + dot_nt(ones, lower)
            write_rows(part, attended)
        return 0

    def write_rows(part, rows):
        for number in range(2):

            @pl.when(part == number)
            def _():
                rows_out[number][...] = rows

    def backward_part(part, _):
        facts = part_facts(part)
        log_total, out_dot = stats[0][part][:1], stats[1][part][:1]
        dq_new = dq_out[0]
        dq_new[part] = jnp.zeros((head_size, lanes), jnp.float32) if finish else dq_in[0][part]

        def differentiate(unit, rows, masked):
            probs = jnp.exp2(scores_of(unit, rows, part, facts, masked) * log2_scale - log_total)
            dprobs = dot_nt(v_scr[unit, rows, :], g_scr[part])
            dscores = (probs * (dprobs - out_dot)).astype(jnp.bfloat16)
            dv_scr[unit, rows, :] += dot_nn(probs.astype(jnp.bfloat16), g_scr[part])
            dk_scr[unit, rows, :] += dot_nn(dscores, q_scr[part])
            dq_new[part] += dot_tn(k_scr[unit, rows, :], dscores)

        each_unit(facts, differentiate)
        if last:
            write_rows(part, (dq_new[part] * scale).T.astype(jnp.bfloat16))
        return 0

    if forward:
        lax.fori_loop(0, 2, forward_part, 0)
    if backward:
        dk_scr[...] = jnp.zeros_like(dk_scr)
        dv_scr[...] = jnp.zeros_like(dv_scr)
        lax.fori_loop(0, 2, backward_part, 0)
        for unit, half, piece, slot in places():
            rows = pl.ds(half * block, block)
            grads[piece][slot, 0] = (dk_scr[unit, rows, :] * scale).astype(jnp.bfloat16)
            grads[piece][slot, 1] = dv_scr[unit, rows, :].astype(jnp.bfloat16)


def run_stage(step, phases, block, group, docs, spot, q_parts, g_parts, pieces, state=(), stats=(), dq=(), after=(), passing=()):
    forward, finish, backward, last = phases
    kind = {0: "own", 4: "far"}.get(step, "pair")
    stage = (kind, *phases)
    units = 4 if kind == "pair" else 2
    y, z = spot
    place = jnp.stack([y, z, jnp.where(z % 2 == 0, step, -step)]).astype(jnp.int32)
    lanes, head_size = q_parts[0].shape
    f32 = lambda *shape: jax.ShapeDtypeStruct(shape, jnp.float32)
    low = lambda array: jax.ShapeDtypeStruct(array.shape, jnp.bfloat16)
    state_shapes = [f32(2, 8, lanes), f32(2, 8, lanes), f32(2, head_size, lanes)]
    dq_shape = f32(2, head_size, lanes)
    operands = [*after, docs, place, *q_parts, *(g_parts if backward else ()), *pieces, *state, *stats, *dq, *passing]
    outs = []
    aliases = {}
    if forward and not finish:
        if state:
            aliases = {len(operands) - 3 + n: n for n in range(3)}
        outs += state_shapes
    if finish or last:
        outs += [low(q) for q in q_parts]
    if finish:
        outs += state_shapes[:2]
    if backward and not last:
        if dq:
            aliases = {len(operands) - 1: len(outs)}
        outs += [dq_shape]
    if backward:
        outs += [low(piece) for piece in pieces]
    for number, array in enumerate(passing):
        aliases[len(operands) - len(passing) + number] = len(outs)
        outs += [low(array)]
    scratch = [
        pltpu.VMEM((units, 2 * block, head_size), jnp.bfloat16),
        pltpu.VMEM((units, 2 * block, head_size), jnp.bfloat16),
        pltpu.VMEM((2, lanes, head_size), jnp.bfloat16),
    ]
    if finish:
        scratch += [pltpu.VMEM(shape.shape, jnp.float32) for shape in state_shapes]
    if backward:
        scratch += [
            pltpu.VMEM((2, lanes, head_size), jnp.bfloat16),
            pltpu.VMEM((units, 2 * block, head_size), jnp.float32),
            pltpu.VMEM((units, 2 * block, head_size), jnp.float32),
        ]
    if last:
        scratch += [pltpu.VMEM(dq_shape.shape, jnp.float32)]
    smem = pl.BlockSpec(memory_space=pltpu.SMEM)
    vmem = pl.BlockSpec(memory_space=pltpu.VMEM)
    anywhere = pl.BlockSpec(memory_space=pl.ANY)
    inside = len(operands) - 2 - len(after) - len(passing)
    products = 2 * forward + 5 * backward
    return pl.pallas_call(
        functools.partial(stage_kernel, stage, len(after), len(passing), block, group),
        out_shape=outs,
        in_specs=[anywhere] * len(after) + [smem, smem] + [vmem] * inside + [anywhere] * len(passing),
        out_specs=[vmem] * (len(outs) - len(passing)) + [anywhere] * len(passing),
        scratch_shapes=scratch,
        input_output_aliases=aliases,
        compiler_params=pltpu.CompilerParams(vmem_limit_bytes=24 * 1024 * 1024),
        cost_estimate=pl.CostEstimate(
            flops=6 * products * 2 * lanes * units * 2 * block * head_size,
            bytes_accessed=4 * 1024 * 1024,
            transcendentals=2 * lanes * units * 2 * block,
        ),
        name="fwd" * forward + "bwd" * backward + kind,
    )(*operands)


def swap_y(mask):
    return [(y * NZ + z, (y ^ mask) * NZ + z) for y in range(NY) for z in range(NZ)]


def swap_z(first):
    turns = [1 if z % 2 == first else -1 for z in range(NZ)]
    return [(y * NZ + z, y * NZ + (z + turns[z]) % NZ) for y in range(NY) for z in range(NZ)]


MIRROR = swap_y(NY - 1)


def add_up(one, other):
    return (one.astype(jnp.float32) + other.astype(jnp.float32)).astype(jnp.bfloat16)


def swap_even(array):
    return lax.ppermute(array, "ctx", swap_z(0))


def swap_odd(array):
    return lax.ppermute(array, "ctx", swap_z(1))


def on_device(queries, key_rows, values, out_grad, doc_lengths):
    block, query_heads, head_size = queries.shape
    key_heads = key_rows.shape[1]
    group = query_heads // key_heads
    place = lax.axis_index("ctx")
    y, z = place // NZ, place % NZ
    mine = y // 2

    def head_of(array, number, width):
        picked = jnp.where(number == 0, array[:, :width], array[:, width:])
        return picked.reshape(block * width, head_size)

    def key_pair(number):
        return jnp.stack([head_of(key_rows, number, 1), head_of(values, number, 1)])

    pairs = [key_pair(mine), key_pair(1 - mine)]
    held = [lax.ppermute(pairs[mask // 2], "ctx", swap_y(mask)) for mask in (1, 3, 2)]
    column = jnp.stack([pairs[0], *held])

    q_parts = [head_of(queries, mine, group), lax.ppermute(head_of(queries, 1 - mine, group), "ctx", MIRROR)]
    g_own, g_leaving = head_of(out_grad, mine, group), head_of(out_grad, 1 - mine, group)
    run = functools.partial(
        run_stage, block=block, group=group, docs=doc_lengths, spot=(y, z), q_parts=q_parts
    )

    evens, odds = [column], [column]
    state = ()
    for step in range(4):
        pieces = [column] if step == 0 else [evens[step], odds[step]]
        if step < 3:
            even, odd = swap_even(odds[step]), swap_odd(evens[step])
        else:
            even, odd = swap_even(odds[step][:2]), swap_odd(evens[step][2:])
        evens.append(even)
        odds.append(odd)
        passing = () if step else (g_leaving,)
        state = run(step, (True, False, False, False), g_parts=(), pieces=pieces, state=state, passing=passing)
        if passing:
            g_parts = [g_own, lax.ppermute(state[3], "ctx", MIRROR)]
            state = state[:3]
    run = functools.partial(run, g_parts=g_parts)
    own_out, other_out, log_total, out_dot, dq, even_grad, odd_grad = run(
        4, (True, True, True, False), pieces=[evens[4], odds[4]], state=state
    )
    stats = (log_total, out_dot)
    other_out = lax.ppermute(other_out, "ctx", MIRROR)
    even, odd = swap_even(even_grad), swap_odd(odd_grad)
    after = ()
    for step in (3, 2, 1):
        dq, even_grad, odd_grad = run(
            step, (False, False, True, False), pieces=[evens[step], odds[step]], stats=stats, dq=(dq,), after=after
        )
        if step == 3:
            odd_grad = jnp.concatenate([add_up(odd_grad[:2], even), odd_grad[2:]], axis=0)
            even_grad = jnp.concatenate([even_grad[:2], add_up(even_grad[2:], odd)], axis=0)
        else:
            odd_grad, even_grad = add_up(odd_grad, even), add_up(even_grad, odd)
        after = (even_grad, odd_grad)
        even, odd = swap_even(even_grad), swap_odd(odd_grad)
    own_dq, other_dq, grad, other_out = run(
        0, (False, False, True, True), pieces=[column], stats=stats, dq=(dq,), after=after, passing=(other_out,)
    )
    other_dq = lax.ppermute(other_dq, "ctx", MIRROR)
    sums = grad.astype(jnp.float32) + even.astype(jnp.float32) + odd.astype(jnp.float32)

    def both_heads(own, other):
        one, two = (r.reshape(block, group, head_size) for r in (own, other))
        return jnp.concatenate([jnp.where(mine == 0, one, two), jnp.where(mine == 0, two, one)], axis=1)

    attended, query_grad = both_heads(own_out, other_out), both_heads(own_dq, other_dq)
    arrived = {
        mask: lax.ppermute(sums[slot].astype(jnp.bfloat16), "ctx", swap_y(mask)).astype(jnp.float32)
        for slot, mask in ((3, 2), (2, 3), (1, 1))
    }
    near, far = sums[0] + arrived[1], arrived[2] + arrived[3]
    heads = [jnp.where(mine == 0, near, far), jnp.where(mine == 0, far, near)]
    grads = jnp.stack(heads, axis=2).astype(jnp.bfloat16)
    return attended, query_grad, grads[0], grads[1]


def solution(mesh):
    placed = (
        P(("dp", "ctx"), "head", None),
        P(("dp", "ctx"), "head", None),
        P(("dp", "ctx"), "head", None),
        P(("dp", "ctx"), "head", None),
        P("dp"),
    )
    return jax.shard_map(
        on_device,
        mesh=mesh,
        in_specs=placed,
        out_specs=(
            P(("dp", "ctx"), "head", None),
            P(("dp", "ctx"), "head", None),
            P(("dp", "ctx"), "head", None),
            P(("dp", "ctx"), "head", None),
        ),
        check_vma=False,
    )
```

```python
import functools
import math

import jax
import jax.numpy as jnp
from jax import lax
from jax.experimental import pallas as pl
from jax.experimental.pallas import tpu as pltpu
from jax.sharding import PartitionSpec as P

MASKED_SCORE = -1e30
NY, NZ = 4, 8


def dot_tn(left, right):
    return lax.dot_general(left, right, (((0,), (0,)), ((), ())), preferred_element_type=jnp.float32)


def dot_nt(left, right):
    return lax.dot_general(left, right, (((1,), (1,)), ((), ())), preferred_element_type=jnp.float32)


def dot_nn(left, right):
    return jnp.dot(left, right, preferred_element_type=jnp.float32)


def stage_kernel(stage, waits, passing, block, group, *refs):
    kind, forward, finish, backward, last = stage
    first = forward and kind == "own"
    paired = kind == "pair"
    units = 4 if paired else 2
    lanes = block * group
    refs = list(refs)
    take = lambda count: [refs.pop(0) for _ in range(count)]
    take(waits)
    docs_ref, place_ref = take(2)
    q_in = take(2)
    g_in = take(2) if backward else []
    pieces = take(1 if kind == "own" else 2)
    state_in = take(3) if forward and not first else []
    stats_in = take(2) if backward and not finish else []
    dq_in = take(1) if backward and not finish else []
    take(passing)
    state_out = take(3) if forward and not finish else []
    rows_out = take(2) if finish or last else []
    stats_out = take(2) if finish else []
    dq_out = take(1) if backward and not last else []
    grads = take(len(pieces)) if backward else []
    take(passing)
    k_scr, v_scr, q_scr = take(3)
    if finish:
        state_out = take(3)
    if backward:
        g_scr, dk_scr, dv_scr = take(3)
    if last:
        dq_out = take(1)
    stats = stats_out or stats_in

    head_size = q_in[0].shape[1]
    scale = 1.0 / math.sqrt(head_size)
    log2_scale = scale * math.log2(math.e)
    y, z, distance = place_ref[0], place_ref[1], place_ref[2]

    def block_of(slot, steps):
        return (y ^ slot ^ (slot >> 1)) * NZ + lax.rem(z + NZ + steps, NZ)

    def blocks_of(unit):
        if paired:
            return block_of(unit, distance), block_of(unit, -distance)
        return block_of(2 * unit, distance), block_of(2 * unit + 1, distance)

    def places():
        for unit in range(units):
            for half in range(2):
                if paired:
                    yield unit, half, half, unit
                else:
                    yield (unit, half, 0, 2 * unit + half) if kind == "own" else (unit, half, unit, half)

    for unit, half, piece, slot in places():
        rows = pl.ds(half * block, block)
        k_scr[unit, rows, :] = pieces[piece][slot, 0]
        v_scr[unit, rows, :] = pieces[piece][slot, 1]
    for part in range(2):
        q_scr[part] = q_in[part][...]
        if backward:
            g_scr[part] = g_in[part][...]

    def doc_start(position):
        bound, start = jnp.int32(0), jnp.zeros_like(position)
        for number in range(docs_ref.shape[0]):
            bound = bound + docs_ref[number]
            start = jnp.where(bound <= position, bound, start)
        return start

    def fold(value):
        return value.reshape(value.shape[0] // 8, 8, value.shape[1])

    def part_facts(part):
        query_block = jnp.where(part == 0, y, NY - 1 - y) * NZ + z
        first_pos = query_block * block
        positions = first_pos + lax.broadcasted_iota(jnp.int32, (1, lanes), 1) // group
        ends = doc_start(first_pos), doc_start(first_pos + block - 1)
        return query_block, *ends, positions, doc_start(positions)

    def is_live(unit, facts):
        query_block, open_first = facts[:2]
        return [(n <= query_block) & ((n + 1) * block > open_first) for n in blocks_of(unit)]

    def is_clear(unit, facts):
        query_block, open_last = facts[0], facts[2]
        one, two = ((n < query_block) & (n * block >= open_last) for n in blocks_of(unit))
        return one & two

    def scores_of(unit, rows, part, facts, masked):
        scores = dot_nt(k_scr[unit, rows, :], q_scr[part])
        if masked:
            one, two = blocks_of(unit)
            row = lax.broadcasted_iota(jnp.int32, scores.shape, 0)
            if scores.shape[0] == block:
                key_pos = row + jnp.where(rows.start == 0, one, two) * block
            else:
                key_pos = row + jnp.where(row < block, one, two - 1) * block
            allowed = (key_pos <= facts[3]) & (key_pos >= facts[4])
            scores = jnp.where(allowed, scores, MASKED_SCORE)
        return scores

    def each_unit(facts, work):
        def step(unit, _):
            one, two = is_live(unit, facts)
            clear = is_clear(unit, facts) & one & two
            whole = pl.ds(0, 2 * block)
            pl.when(clear)(lambda: work(unit, whole, False))
            if kind == "own":

                def half_step(half, _):
                    live = jnp.where(half == 0, one, two) & jnp.logical_not(clear)
                    rows = pl.ds(pl.multiple_of(half * block, block), block)
                    pl.when(live)(lambda: work(unit, rows, True))
                    return 0

                lax.fori_loop(0, 2, half_step, 0)
                return 0
            pl.when(one & two & jnp.logical_not(clear))(lambda: work(unit, whole, True))
            half = pl.ds(pl.multiple_of(jnp.where(one, 0, block), block), block)
            pl.when(one ^ two)(lambda: work(unit, half, True))
            return 0

        lax.fori_loop(0, units, step, 0)

    def forward_part(part, _):
        facts = part_facts(part)
        m_new, l_new, o_new = state_out
        if first:
            m_new[part] = jnp.full((8, lanes), MASKED_SCORE, jnp.float32)
            l_new[part] = jnp.zeros((8, lanes), jnp.float32)
            o_new[part] = jnp.zeros((head_size, lanes), jnp.float32)
        else:
            for old, new in zip(state_in, state_out):
                new[part] = old[part]

        def attend(unit, rows, masked):
            scores = scores_of(unit, rows, part, facts, masked)
            m_old = m_new[part]
            top = jnp.maximum(m_old, jnp.max(scores, axis=0, keepdims=True))
            fading = jnp.exp2((m_old - top) * log2_scale)
            weights = jnp.exp2(scores * log2_scale - top[:1] * log2_scale)
            m_new[part] = top
            l_new[part] = l_new[part] * fading + jnp.sum(fold(weights), axis=0)
            added = dot_tn(v_scr[unit, rows, :], weights.astype(jnp.bfloat16))
            o_new[part] = o_new[part] * fading[:1] + added

        each_unit(facts, attend)
        row_max = m_new[part][:1] * log2_scale
        if finish:
            row_total = jnp.sum(l_new[part], axis=0, keepdims=True)
            attended = (o_new[part] / row_total).T.astype(jnp.bfloat16)
            products = attended.astype(jnp.float32) * g_scr[part].astype(jnp.float32)
            stats_out[0][part] = jnp.broadcast_to(row_max + jnp.log2(row_total), (8, lanes))
            upper = products.astype(jnp.bfloat16)
            lower = (products - upper.astype(jnp.float32)).astype(jnp.bfloat16)
            ones = jnp.ones((8, head_size), jnp.bfloat16)
            stats_out[1][part] = dot_nt(ones, upper) + dot_nt(ones, lower)
            write_rows(part, attended)
        return 0

    def write_rows(part, rows):
        for number in range(2):

            @pl.when(part == number)
            def _():
                rows_out[number][...] = rows

    def backward_part(part, _):
        facts = part_facts(part)
        log_total, out_dot = stats[0][part][:1], stats[1][part][:1]
        dq_new = dq_out[0]
        dq_new[part] = jnp.zeros((head_size, lanes), jnp.float32) if finish else dq_in[0][part]

        def differentiate(unit, rows, masked):
            probs = jnp.exp2(scores_of(unit, rows, part, facts, masked) * log2_scale - log_total)
            dprobs = dot_nt(v_scr[unit, rows, :], g_scr[part])
            dscores = (probs * (dprobs - out_dot)).astype(jnp.bfloat16)
            dv_scr[unit, rows, :] += dot_nn(probs.astype(jnp.bfloat16), g_scr[part])
            dk_scr[unit, rows, :] += dot_nn(dscores, q_scr[part])
            dq_new[part] += dot_tn(k_scr[unit, rows, :], dscores)

        each_unit(facts, differentiate)
        if last:
            write_rows(part, (dq_new[part] * scale).T.astype(jnp.bfloat16))
        return 0

    if forward:
        lax.fori_loop(0, 2, forward_part, 0)
    if backward:
        dk_scr[...] = jnp.zeros_like(dk_scr)
        dv_scr[...] = jnp.zeros_like(dv_scr)
        lax.fori_loop(0, 2, backward_part, 0)
        for unit, half, piece, slot in places():
            rows = pl.ds(half * block, block)
            grads[piece][slot, 0] = (dk_scr[unit, rows, :] * scale).astype(jnp.bfloat16)
            grads[piece][slot, 1] = dv_scr[unit, rows, :].astype(jnp.bfloat16)


def run_stage(step, phases, block, group, docs, spot, q_parts, g_parts, pieces, state=(), stats=(), dq=(), after=(), passing=()):
    forward, finish, backward, last = phases
    kind = {0: "own", 4: "far"}.get(step, "pair")
    stage = (kind, *phases)
    units = 4 if kind == "pair" else 2
    y, z = spot
    place = jnp.stack([y, z, jnp.where(z % 2 == 0, step, -step)]).astype(jnp.int32)
    lanes, head_size = q_parts[0].shape
    f32 = lambda *shape: jax.ShapeDtypeStruct(shape, jnp.float32)
    low = lambda array: jax.ShapeDtypeStruct(array.shape, jnp.bfloat16)
    state_shapes = [f32(2, 8, lanes), f32(2, 8, lanes), f32(2, head_size, lanes)]
    dq_shape = f32(2, head_size, lanes)
    operands = [*after, docs, place, *q_parts, *(g_parts if backward else ()), *pieces, *state, *stats, *dq, *passing]
    outs = []
    aliases = {}
    if forward and not finish:
        if state:
            aliases = {len(operands) - 3 + n: n for n in range(3)}
        outs += state_shapes
    if finish or last:
        outs += [low(q) for q in q_parts]
    if finish:
        outs += state_shapes[:2]
    if backward and not last:
        if dq:
            aliases = {len(operands) - 1: len(outs)}
        outs += [dq_shape]
    if backward:
        outs += [low(piece) for piece in pieces]
    for number, array in enumerate(passing):
        aliases[len(operands) - len(passing) + number] = len(outs)
        outs += [low(array)]
    scratch = [
        pltpu.VMEM((units, 2 * block, head_size), jnp.bfloat16),
        pltpu.VMEM((units, 2 * block, head_size), jnp.bfloat16),
        pltpu.VMEM((2, lanes, head_size), jnp.bfloat16),
    ]
    if finish:
        scratch += [pltpu.VMEM(shape.shape, jnp.float32) for shape in state_shapes]
    if backward:
        scratch += [
            pltpu.VMEM((2, lanes, head_size), jnp.bfloat16),
            pltpu.VMEM((units, 2 * block, head_size), jnp.float32),
            pltpu.VMEM((units, 2 * block, head_size), jnp.float32),
        ]
    if last:
        scratch += [pltpu.VMEM(dq_shape.shape, jnp.float32)]
    smem = pl.BlockSpec(memory_space=pltpu.SMEM)
    vmem = pl.BlockSpec(memory_space=pltpu.VMEM)
    anywhere = pl.BlockSpec(memory_space=pl.ANY)
    inside = len(operands) - 2 - len(after) - len(passing)
    products = 2 * forward + 5 * backward
    return pl.pallas_call(
        functools.partial(stage_kernel, stage, len(after), len(passing), block, group),
        out_shape=outs,
        in_specs=[anywhere] * len(after) + [smem, smem] + [vmem] * inside + [anywhere] * len(passing),
        out_specs=[vmem] * (len(outs) - len(passing)) + [anywhere] * len(passing),
        scratch_shapes=scratch,
        input_output_aliases=aliases,
        compiler_params=pltpu.CompilerParams(vmem_limit_bytes=24 * 1024 * 1024),
        cost_estimate=pl.CostEstimate(
            flops=6 * products * 2 * lanes * units * 2 * block * head_size,
            bytes_accessed=4 * 1024 * 1024,
            transcendentals=2 * lanes * units * 2 * block,
        ),
        name="fwd" * forward + "bwd" * backward + kind,
    )(*operands)


def swap_y(mask):
    return [(y * NZ + z, (y ^ mask) * NZ + z) for y in range(NY) for z in range(NZ)]


def swap_z(first):
    turns = [1 if z % 2 == first else -1 for z in range(NZ)]
    return [(y * NZ + z, y * NZ + (z + turns[z]) % NZ) for y in range(NY) for z in range(NZ)]


MIRROR = swap_y(NY - 1)


def add_up(one, other):
    return (one.astype(jnp.float32) + other.astype(jnp.float32)).astype(jnp.bfloat16)


def swap_even(array):
    return lax.ppermute(array, "ctx", swap_z(0))


def swap_odd(array):
    return lax.ppermute(array, "ctx", swap_z(1))


def on_device(queries, key_rows, values, out_grad, doc_lengths):
    block, query_heads, head_size = queries.shape
    key_heads = key_rows.shape[1]
    group = query_heads // key_heads
    place = lax.axis_index("ctx")
    y, z = place // NZ, place % NZ
    mine = y // 2

    def head_of(array, number, width):
        picked = jnp.where(number == 0, array[:, :width], array[:, width:])
        return picked.reshape(block * width, head_size)

    def key_pair(number):
        return jnp.stack([head_of(key_rows, number, 1), head_of(values, number, 1)])

    pairs = [key_pair(mine), key_pair(1 - mine)]
    held = [lax.ppermute(pairs[mask // 2], "ctx", swap_y(mask)) for mask in (1, 3, 2)]
    column = jnp.stack([pairs[0], *held])

    q_parts = [head_of(queries, mine, group), lax.ppermute(head_of(queries, 1 - mine, group), "ctx", MIRROR)]
    g_own, g_leaving = head_of(out_grad, mine, group), head_of(out_grad, 1 - mine, group)
    run = functools.partial(
        run_stage, block=block, group=group, docs=doc_lengths, spot=(y, z), q_parts=q_parts
    )

    evens, odds = [column], [column]
    state = ()
    for step in range(4):
        pieces = [column] if step == 0 else [evens[step], odds[step]]
        if step < 3:
            even, odd = swap_even(odds[step]), swap_odd(evens[step])
        else:
            even, odd = swap_even(odds[step][:2]), swap_odd(evens[step][2:])
        evens.append(even)
        odds.append(odd)
        passing = () if step else (g_leaving,)
        state = run(step, (True, False, False, False), g_parts=(), pieces=pieces, state=state, passing=passing)
        if passing:
            g_parts = [g_own, lax.ppermute(state[3], "ctx", MIRROR)]
            state = state[:3]
    run = functools.partial(run, g_parts=g_parts)
    own_out, other_out, log_total, out_dot, dq, even_grad, odd_grad = run(
        4, (True, True, True, False), pieces=[evens[4], odds[4]], state=state
    )
    stats = (log_total, out_dot)
    other_out = lax.ppermute(other_out, "ctx", MIRROR)
    even, odd = swap_even(even_grad), swap_odd(odd_grad)
    after = ()
    for step in (3, 2, 1):
        dq, even_grad, odd_grad = run(
            step, (False, False, True, False), pieces=[evens[step], odds[step]], stats=stats, dq=(dq,), after=after
        )
        if step == 3:
            odd_grad = jnp.concatenate([add_up(odd_grad[:2], even), odd_grad[2:]], axis=0)
            even_grad = jnp.concatenate([even_grad[:2], add_up(even_grad[2:], odd)], axis=0)
        else:
            odd_grad, even_grad = add_up(odd_grad, even), add_up(even_grad, odd)
        after = (even_grad, odd_grad)
        even, odd = swap_even(even_grad), swap_odd(odd_grad)
    own_dq, other_dq, grad, other_out = run(
        0, (False, False, True, True), pieces=[column], stats=stats, dq=(dq,), after=after, passing=(other_out,)
    )
    other_dq = lax.ppermute(other_dq, "ctx", MIRROR)
    sums = grad.astype(jnp.float32) + even.astype(jnp.float32) + odd.astype(jnp.float32)

    def both_heads(own, other):
        one, two = (r.reshape(block, group, head_size) for r in (own, other))
        return jnp.concatenate([jnp.where(mine == 0, one, two), jnp.where(mine == 0, two, one)], axis=1)

    attended, query_grad = both_heads(own_out, other_out), both_heads(own_dq, other_dq)
    arrived = {
        mask: lax.ppermute(sums[slot].astype(jnp.bfloat16), "ctx", swap_y(mask)).astype(jnp.float32)
        for slot, mask in ((3, 2), (2, 3), (1, 1))
    }
    near, far = sums[0] + arrived[1], arrived[2] + arrived[3]
    heads = [jnp.where(mine == 0, near, far), jnp.where(mine == 0, far, near)]
    grads = jnp.stack(heads, axis=2).astype(jnp.bfloat16)
    return attended, query_grad, grads[0], grads[1]


def solution(mesh):
    placed = (
        P(("dp", "ctx"), "head", None),
        P(("dp", "ctx"), "head", None),
        P(("dp", "ctx"), "head", None),
        P(("dp", "ctx"), "head", None),
        P("dp"),
    )
    return jax.shard_map(
        on_device,
        mesh=mesh,
        in_specs=placed,
        out_specs=(
            P(("dp", "ctx"), "head", None),
            P(("dp", "ctx"), "head", None),
            P(("dp", "ctx"), "head", None),
            P(("dp", "ctx"), "head", None),
        ),
        check_vma=False,
    )
```

```python
import functools
import math

import jax
import jax.numpy as jnp
from jax import lax
from jax.experimental import pallas as pl
from jax.experimental.pallas import tpu as pltpu
from jax.sharding import PartitionSpec as P

MASKED_SCORE = -1e30
NY, NZ = 4, 8


def dot_tn(left, right):
    return lax.dot_general(left, right, (((0,), (0,)), ((), ())), preferred_element_type=jnp.float32)


def dot_nt(left, right):
    return lax.dot_general(left, right, (((1,), (1,)), ((), ())), preferred_element_type=jnp.float32)


def dot_nn(left, right):
    return jnp.dot(left, right, preferred_element_type=jnp.float32)


def stage_kernel(stage, waits, passing, block, group, *refs):
    kind, forward, finish, backward, last = stage
    first = forward and kind == "own"
    paired = kind == "pair"
    units = 4 if paired else 2
    lanes = block * group
    refs = list(refs)
    take = lambda count: [refs.pop(0) for _ in range(count)]
    take(waits)
    docs_ref, place_ref = take(2)
    q_in = take(2)
    g_in = take(2) if backward else []
    pieces = take(1 if kind == "own" else 2)
    state_in = take(3) if forward and not first else []
    stats_in = take(2) if backward and not finish else []
    dq_in = take(1) if backward and not finish else []
    take(passing)
    state_out = take(3) if forward and not finish else []
    rows_out = take(2) if finish or last else []
    stats_out = take(2) if finish else []
    dq_out = take(1) if backward and not last else []
    grads = take(len(pieces)) if backward else []
    take(passing)
    k_scr, v_scr, q_scr = take(3)
    if finish:
        state_out = take(3)
    if backward:
        g_scr, dk_scr, dv_scr = take(3)
    if last:
        dq_out = take(1)
    stats = stats_out or stats_in

    head_size = q_in[0].shape[1]
    scale = 1.0 / math.sqrt(head_size)
    log2_scale = scale * math.log2(math.e)
    y, z, distance = place_ref[0], place_ref[1], place_ref[2]

    def block_of(slot, steps):
        return (y ^ slot ^ (slot >> 1)) * NZ + lax.rem(z + NZ + steps, NZ)

    def blocks_of(unit):
        if paired:
            return block_of(unit, distance), block_of(unit, -distance)
        return block_of(2 * unit, distance), block_of(2 * unit + 1, distance)

    def places():
        for unit in range(units):
            for half in range(2):
                if paired:
                    yield unit, half, half, unit
                else:
                    yield (unit, half, 0, 2 * unit + half) if kind == "own" else (unit, half, unit, half)

    for unit, half, piece, slot in places():
        rows = pl.ds(half * block, block)
        k_scr[unit, rows, :] = pieces[piece][slot, 0]
        v_scr[unit, rows, :] = pieces[piece][slot, 1]
    for part in range(2):
        q_scr[part] = q_in[part][...]
        if backward:
            g_scr[part] = g_in[part][...]

    def doc_start(position):
        bound, start = jnp.int32(0), jnp.zeros_like(position)
        for number in range(docs_ref.shape[0]):
            bound = bound + docs_ref[number]
            start = jnp.where(bound <= position, bound, start)
        return start

    def fold(value):
        return value.reshape(value.shape[0] // 8, 8, value.shape[1])

    def part_facts(part):
        query_block = jnp.where(part == 0, y, NY - 1 - y) * NZ + z
        first_pos = query_block * block
        positions = first_pos + lax.broadcasted_iota(jnp.int32, (1, lanes), 1) // group
        ends = doc_start(first_pos), doc_start(first_pos + block - 1)
        return query_block, *ends, positions, doc_start(positions)

    def is_live(unit, facts):
        query_block, open_first = facts[:2]
        return [(n <= query_block) & ((n + 1) * block > open_first) for n in blocks_of(unit)]

    def is_clear(unit, facts):
        query_block, open_last = facts[0], facts[2]
        one, two = ((n < query_block) & (n * block >= open_last) for n in blocks_of(unit))
        return one & two

    def scores_of(unit, rows, part, facts, masked):
        scores = dot_nt(k_scr[unit, rows, :], q_scr[part])
        if masked:
            one, two = blocks_of(unit)
            row = lax.broadcasted_iota(jnp.int32, scores.shape, 0)
            if scores.shape[0] == block:
                key_pos = row + jnp.where(rows.start == 0, one, two) * block
            else:
                key_pos = row + jnp.where(row < block, one, two - 1) * block
            allowed = (key_pos <= facts[3]) & (key_pos >= facts[4])
            scores = jnp.where(allowed, scores, MASKED_SCORE)
        return scores

    def each_unit(facts, work):
        def step(unit, _):
            one, two = is_live(unit, facts)
            both, whole = one & two, pl.ds(0, 2 * block)
            if kind == "own":
                pl.when(both)(lambda: work(unit, whole, True))
            else:
                clear = is_clear(unit, facts)
                pl.when(both & clear)(lambda: work(unit, whole, False))
                pl.when(both & jnp.logical_not(clear))(lambda: work(unit, whole, True))
            half = pl.ds(pl.multiple_of(jnp.where(one, 0, block), block), block)
            pl.when(one ^ two)(lambda: work(unit, half, True))
            return 0

        lax.fori_loop(0, units, step, 0)

    def forward_part(part, _):
        facts = part_facts(part)
        m_new, l_new, o_new = state_out
        if first:
            m_new[part] = jnp.full((8, lanes), MASKED_SCORE, jnp.float32)
            l_new[part] = jnp.zeros((8, lanes), jnp.float32)
            o_new[part] = jnp.zeros((head_size, lanes), jnp.float32)
        else:
            for old, new in zip(state_in, state_out):
                new[part] = old[part]

        def attend(unit, rows, masked):
            scores = scores_of(unit, rows, part, facts, masked)
            m_old = m_new[part]
            top = jnp.maximum(m_old, jnp.max(scores, axis=0, keepdims=True))
            fading = jnp.exp2((m_old - top) * log2_scale)
            weights = jnp.exp2(scores * log2_scale - top[:1] * log2_scale)
            m_new[part] = top
            l_new[part] = l_new[part] * fading + jnp.sum(fold(weights), axis=0)
            added = dot_tn(v_scr[unit, rows, :], weights.astype(jnp.bfloat16))
            o_new[part] = o_new[part] * fading[:1] + added

        each_unit(facts, attend)
        row_max = m_new[part][:1] * log2_scale
        if finish:
            row_total = jnp.sum(l_new[part], axis=0, keepdims=True)
            attended = (o_new[part] / row_total).T.astype(jnp.bfloat16)
            products = attended.astype(jnp.float32) * g_scr[part].astype(jnp.float32)
            stats_out[0][part] = jnp.broadcast_to(row_max + jnp.log2(row_total), (8, lanes))
            upper = products.astype(jnp.bfloat16)
            lower = (products - upper.astype(jnp.float32)).astype(jnp.bfloat16)
            ones = jnp.ones((8, head_size), jnp.bfloat16)
            stats_out[1][part] = dot_nt(ones, upper) + dot_nt(ones, lower)
            write_rows(part, attended)
        return 0

    def write_rows(part, rows):
        for number in range(2):

            @pl.when(part == number)
            def _():
                rows_out[number][...] = rows

    def backward_part(part, _):
        facts = part_facts(part)
        log_total, out_dot = stats[0][part][:1], stats[1][part][:1]
        dq_new = dq_out[0]
        dq_new[part] = jnp.zeros((head_size, lanes), jnp.float32) if finish else dq_in[0][part]

        def differentiate(unit, rows, masked):
            probs = jnp.exp2(scores_of(unit, rows, part, facts, masked) * log2_scale - log_total)
            dprobs = dot_nt(v_scr[unit, rows, :], g_scr[part])
            dscores = (probs * (dprobs - out_dot)).astype(jnp.bfloat16)
            dv_scr[unit, rows, :] += dot_nn(probs.astype(jnp.bfloat16), g_scr[part])
            dk_scr[unit, rows, :] += dot_nn(dscores, q_scr[part])
            dq_new[part] += dot_tn(k_scr[unit, rows, :], dscores)

        each_unit(facts, differentiate)
        if last:
            write_rows(part, (dq_new[part] * scale).T.astype(jnp.bfloat16))
        return 0

    if forward:
        lax.fori_loop(0, 2, forward_part, 0)
    if backward:
        dk_scr[...] = jnp.zeros_like(dk_scr)
        dv_scr[...] = jnp.zeros_like(dv_scr)
        lax.fori_loop(0, 2, backward_part, 0)
        for unit, half, piece, slot in places():
            rows = pl.ds(half * block, block)
            grads[piece][slot, 0] = (dk_scr[unit, rows, :] * scale).astype(jnp.bfloat16)
            grads[piece][slot, 1] = dv_scr[unit, rows, :].astype(jnp.bfloat16)


def run_stage(step, phases, block, group, docs, spot, q_parts, g_parts, pieces, state=(), stats=(), dq=(), after=(), passing=()):
    forward, finish, backward, last = phases
    kind = {0: "own", 4: "far"}.get(step, "pair")
    stage = (kind, *phases)
    units = 4 if kind == "pair" else 2
    y, z = spot
    place = jnp.stack([y, z, jnp.where(z % 2 == 0, step, -step)]).astype(jnp.int32)
    lanes, head_size = q_parts[0].shape
    f32 = lambda *shape: jax.ShapeDtypeStruct(shape, jnp.float32)
    low = lambda array: jax.ShapeDtypeStruct(array.shape, jnp.bfloat16)
    state_shapes = [f32(2, 8, lanes), f32(2, 8, lanes), f32(2, head_size, lanes)]
    dq_shape = f32(2, head_size, lanes)
    operands = [*after, docs, place, *q_parts, *(g_parts if backward else ()), *pieces, *state, *stats, *dq, *passing]
    outs = []
    aliases = {}
    if forward and not finish:
        if state:
            aliases = {len(operands) - 3 + n: n for n in range(3)}
        outs += state_shapes
    if finish or last:
        outs += [low(q) for q in q_parts]
    if finish:
        outs += state_shapes[:2]
    if backward and not last:
        if dq:
            aliases = {len(operands) - 1: len(outs)}
        outs += [dq_shape]
    if backward:
        outs += [low(piece) for piece in pieces]
    for number, array in enumerate(passing):
        aliases[len(operands) - len(passing) + number] = len(outs)
        outs += [low(array)]
    scratch = [
        pltpu.VMEM((units, 2 * block, head_size), jnp.bfloat16),
        pltpu.VMEM((units, 2 * block, head_size), jnp.bfloat16),
        pltpu.VMEM((2, lanes, head_size), jnp.bfloat16),
    ]
    if finish:
        scratch += [pltpu.VMEM(shape.shape, jnp.float32) for shape in state_shapes]
    if backward:
        scratch += [
            pltpu.VMEM((2, lanes, head_size), jnp.bfloat16),
            pltpu.VMEM((units, 2 * block, head_size), jnp.float32),
            pltpu.VMEM((units, 2 * block, head_size), jnp.float32),
        ]
    if last:
        scratch += [pltpu.VMEM(dq_shape.shape, jnp.float32)]
    smem = pl.BlockSpec(memory_space=pltpu.SMEM)
    vmem = pl.BlockSpec(memory_space=pltpu.VMEM)
    anywhere = pl.BlockSpec(memory_space=pl.ANY)
    inside = len(operands) - 2 - len(after) - len(passing)
    products = 2 * forward + 5 * backward
    return pl.pallas_call(
        functools.partial(stage_kernel, stage, len(after), len(passing), block, group),
        out_shape=outs,
        in_specs=[anywhere] * len(after) + [smem, smem] + [vmem] * inside + [anywhere] * len(passing),
        out_specs=[vmem] * (len(outs) - len(passing)) + [anywhere] * len(passing),
        scratch_shapes=scratch,
        input_output_aliases=aliases,
        compiler_params=pltpu.CompilerParams(vmem_limit_bytes=24 * 1024 * 1024),
        cost_estimate=pl.CostEstimate(
            flops=6 * products * 2 * lanes * units * 2 * block * head_size,
            bytes_accessed=4 * 1024 * 1024,
            transcendentals=2 * lanes * units * 2 * block,
        ),
        name="fwd" * forward + "bwd" * backward + kind,
    )(*operands)


def swap_y(mask):
    return [(y * NZ + z, (y ^ mask) * NZ + z) for y in range(NY) for z in range(NZ)]


def swap_z(first):
    turns = [1 if z % 2 == first else -1 for z in range(NZ)]
    return [(y * NZ + z, y * NZ + (z + turns[z]) % NZ) for y in range(NY) for z in range(NZ)]


MIRROR = swap_y(NY - 1)


def add_up(one, other):
    return (one.astype(jnp.float32) + other.astype(jnp.float32)).astype(jnp.bfloat16)


def swap_even(array):
    return lax.ppermute(array, "ctx", swap_z(0))


def swap_odd(array):
    return lax.ppermute(array, "ctx", swap_z(1))


def on_device(queries, key_rows, values, out_grad, doc_lengths):
    block, query_heads, head_size = queries.shape
    key_heads = key_rows.shape[1]
    group = query_heads // key_heads
    place = lax.axis_index("ctx")
    y, z = place // NZ, place % NZ
    mine = y // 2

    def head_of(array, number, width):
        picked = jnp.where(number == 0, array[:, :width], array[:, width:])
        return picked.reshape(block * width, head_size)

    def key_pair(number):
        return jnp.stack([head_of(key_rows, number, 1), head_of(values, number, 1)])

    pairs = [key_pair(mine), key_pair(1 - mine)]
    held = [lax.ppermute(pairs[mask // 2], "ctx", swap_y(mask)) for mask in (1, 3, 2)]
    column = jnp.stack([pairs[0], *held])

    q_parts = [head_of(queries, mine, group), lax.ppermute(head_of(queries, 1 - mine, group), "ctx", MIRROR)]
    g_own, g_leaving = head_of(out_grad, mine, group), head_of(out_grad, 1 - mine, group)
    run = functools.partial(
        run_stage, block=block, group=group, docs=doc_lengths, spot=(y, z), q_parts=q_parts
    )

    evens, odds = [column], [column]
    state = ()
    for step in range(4):
        pieces = [column] if step == 0 else [evens[step], odds[step]]
        if step < 3:
            even, odd = swap_even(odds[step]), swap_odd(evens[step])
        else:
            even, odd = swap_even(odds[step][:2]), swap_odd(evens[step][2:])
        evens.append(even)
        odds.append(odd)
        passing = () if step else (g_leaving,)
        state = run(step, (True, False, False, False), g_parts=(), pieces=pieces, state=state, passing=passing)
        if passing:
            g_parts = [g_own, lax.ppermute(state[3], "ctx", MIRROR)]
            state = state[:3]
    run = functools.partial(run, g_parts=g_parts)
    own_out, other_out, log_total, out_dot, dq, even_grad, odd_grad = run(
        4, (True, True, True, False), pieces=[evens[4], odds[4]], state=state
    )
    stats = (log_total, out_dot)
    other_out = lax.ppermute(other_out, "ctx", MIRROR)
    even, odd = swap_even(even_grad), swap_odd(odd_grad)
    after = ()
    for step in (3, 2, 1):
        dq, even_grad, odd_grad = run(
            step, (False, False, True, False), pieces=[evens[step], odds[step]], stats=stats, dq=(dq,), after=after
        )
        if step == 3:
            odd_grad = jnp.concatenate([add_up(odd_grad[:2], even), odd_grad[2:]], axis=0)
            even_grad = jnp.concatenate([even_grad[:2], add_up(even_grad[2:], odd)], axis=0)
        else:
            odd_grad, even_grad = add_up(odd_grad, even), add_up(even_grad, odd)
        after = (even_grad, odd_grad)
        even, odd = swap_even(even_grad), swap_odd(odd_grad)
    own_dq, other_dq, grad, other_out = run(
        0, (False, False, True, True), pieces=[column], stats=stats, dq=(dq,), after=after, passing=(other_out,)
    )
    other_dq = lax.ppermute(other_dq, "ctx", MIRROR)
    sums = grad.astype(jnp.float32) + even.astype(jnp.float32) + odd.astype(jnp.float32)

    def both_heads(own, other):
        one, two = (r.reshape(block, group, head_size) for r in (own, other))
        return jnp.concatenate([jnp.where(mine == 0, one, two), jnp.where(mine == 0, two, one)], axis=1)

    attended, query_grad = both_heads(own_out, other_out), both_heads(own_dq, other_dq)
    arrived = {
        mask: lax.ppermute(sums[slot].astype(jnp.bfloat16), "ctx", swap_y(mask)).astype(jnp.float32)
        for slot, mask in ((3, 2), (2, 3), (1, 1))
    }
    near, far = sums[0] + arrived[1], arrived[2] + arrived[3]
    heads = [jnp.where(mine == 0, near, far), jnp.where(mine == 0, far, near)]
    grads = jnp.stack(heads, axis=2).astype(jnp.bfloat16)
    return attended, query_grad, grads[0], grads[1]


def solution(mesh):
    placed = (
        P(("dp", "ctx"), "head", None),
        P(("dp", "ctx"), "head", None),
        P(("dp", "ctx"), "head", None),
        P(("dp", "ctx"), "head", None),
        P("dp"),
    )
    return jax.shard_map(
        on_device,
        mesh=mesh,
        in_specs=placed,
        out_specs=(
            P(("dp", "ctx"), "head", None),
            P(("dp", "ctx"), "head", None),
            P(("dp", "ctx"), "head", None),
            P(("dp", "ctx"), "head", None),
        ),
        check_vma=False,
    )
```

```python
import functools
import math

import jax
import jax.numpy as jnp
from jax import lax
from jax.experimental import pallas as pl
from jax.experimental.pallas import tpu as pltpu
from jax.sharding import PartitionSpec as P

MASKED_SCORE = -1e30
NY, NZ = 4, 8


def dot_tn(left, right):
    return lax.dot_general(left, right, (((0,), (0,)), ((), ())), preferred_element_type=jnp.float32)


def dot_nt(left, right):
    return lax.dot_general(left, right, (((1,), (1,)), ((), ())), preferred_element_type=jnp.float32)


def dot_nn(left, right):
    return jnp.dot(left, right, preferred_element_type=jnp.float32)


def stage_kernel(stage, waits, passing, block, group, *refs):
    kind, forward, finish, backward, last = stage
    first = forward and kind == "own"
    paired = kind == "pair"
    units = 4 if paired else 2
    lanes = block * group
    refs = list(refs)
    take = lambda count: [refs.pop(0) for _ in range(count)]
    take(waits)
    docs_ref, place_ref = take(2)
    q_in = take(2)
    g_in = take(2) if backward else []
    pieces = take(1 if kind == "own" else 2)
    state_in = take(3) if forward and not first else []
    stats_in = take(2) if backward and not finish else []
    dq_in = take(1) if backward and not finish else []
    take(passing)
    state_out = take(3) if forward and not finish else []
    rows_out = take(2) if finish or last else []
    stats_out = take(2) if finish else []
    dq_out = take(1) if backward and not last else []
    grads = take(len(pieces)) if backward else []
    take(passing)
    k_scr, v_scr, q_scr = take(3)
    if finish:
        state_out = take(3)
    if backward:
        g_scr, dk_scr, dv_scr = take(3)
    if last:
        dq_out = take(1)
    stats = stats_out or stats_in

    head_size = q_in[0].shape[1]
    scale = 1.0 / math.sqrt(head_size)
    log2_scale = scale * math.log2(math.e)
    y, z, distance = place_ref[0], place_ref[1], place_ref[2]

    def block_of(slot, steps):
        return (y ^ slot ^ (slot >> 1)) * NZ + lax.rem(z + NZ + steps, NZ)

    def blocks_of(unit):
        if paired:
            return block_of(unit, distance), block_of(unit, -distance)
        return block_of(2 * unit, distance), block_of(2 * unit + 1, distance)

    def places():
        for unit in range(units):
            for half in range(2):
                if paired:
                    yield unit, half, half, unit
                else:
                    yield (unit, half, 0, 2 * unit + half) if kind == "own" else (unit, half, unit, half)

    for unit, half, piece, slot in places():
        rows = pl.ds(half * block, block)
        k_scr[unit, rows, :] = pieces[piece][slot, 0]
        v_scr[unit, rows, :] = pieces[piece][slot, 1]
    for part in range(2):
        q_scr[part] = q_in[part][...]
        if backward:
            g_scr[part] = g_in[part][...]

    def doc_start(position):
        bound, start = jnp.int32(0), jnp.zeros_like(position)
        for number in range(docs_ref.shape[0]):
            bound = bound + docs_ref[number]
            start = jnp.where(bound <= position, bound, start)
        return start

    def fold(value):
        return value.reshape(value.shape[0] // 8, 8, value.shape[1])

    def part_facts(part):
        query_block = jnp.where(part == 0, y, NY - 1 - y) * NZ + z
        first_pos = query_block * block
        positions = first_pos + lax.broadcasted_iota(jnp.int32, (1, lanes), 1) // group
        ends = doc_start(first_pos), doc_start(first_pos + block - 1)
        return query_block, *ends, positions, doc_start(positions)

    def is_live(unit, facts):
        query_block, open_first = facts[:2]
        return [(n <= query_block) & ((n + 1) * block > open_first) for n in blocks_of(unit)]

    def is_clear(unit, facts):
        query_block, open_last = facts[0], facts[2]
        one, two = ((n < query_block) & (n * block >= open_last) for n in blocks_of(unit))
        return one & two

    def scores_of(unit, rows, part, facts, masked):
        scores = dot_nt(k_scr[unit, rows, :], q_scr[part])
        if masked:
            one, two = blocks_of(unit)
            row = lax.broadcasted_iota(jnp.int32, scores.shape, 0)
            if scores.shape[0] == block:
                key_pos = row + jnp.where(rows.start == 0, one, two) * block
            else:
                key_pos = row + jnp.where(row < block, one, two - 1) * block
            allowed = (key_pos <= facts[3]) & (key_pos >= facts[4])
            scores = jnp.where(allowed, scores, MASKED_SCORE)
        return scores

    def each_unit(facts, work):
        def step(unit, _):
            one, two = is_live(unit, facts)
            both, whole = one & two, pl.ds(0, 2 * block)
            if kind == "own":
                pl.when(both)(lambda: work(unit, whole, True))
            else:
                clear = is_clear(unit, facts)
                pl.when(both & clear)(lambda: work(unit, whole, False))
                pl.when(both & jnp.logical_not(clear))(lambda: work(unit, whole, True))
            half = pl.ds(pl.multiple_of(jnp.where(one, 0, block), block), block)
            pl.when(one ^ two)(lambda: work(unit, half, True))
            return 0

        lax.fori_loop(0, units, step, 0)

    def forward_part(part, _):
        facts = part_facts(part)
        m_new, l_new, o_new = state_out
        if first:
            m_new[part] = jnp.full((8, lanes), MASKED_SCORE, jnp.float32)
            l_new[part] = jnp.zeros((8, lanes), jnp.float32)
            o_new[part] = jnp.zeros((head_size, lanes), jnp.float32)
        else:
            for old, new in zip(state_in, state_out):
                new[part] = old[part]

        def attend(unit, rows, masked):
            scores = scores_of(unit, rows, part, facts, masked)
            m_old = m_new[part]
            top = jnp.maximum(m_old, jnp.max(scores, axis=0, keepdims=True))
            fading = jnp.exp2((m_old - top) * log2_scale)
            weights = jnp.exp2(scores * log2_scale - top[:1] * log2_scale)
            m_new[part] = top
            l_new[part] = l_new[part] * fading + jnp.sum(fold(weights), axis=0)
            added = dot_tn(v_scr[unit, rows, :], weights.astype(jnp.bfloat16))
            o_new[part] = o_new[part] * fading[:1] + added

        each_unit(facts, attend)
        row_max = m_new[part][:1] * log2_scale
        if finish:
            row_total = jnp.sum(l_new[part], axis=0, keepdims=True)
            attended = (o_new[part] / row_total).T.astype(jnp.bfloat16)
            products = attended.astype(jnp.float32) * g_scr[part].astype(jnp.float32)
            stats_out[0][part] = jnp.broadcast_to(row_max + jnp.log2(row_total), (8, lanes))
            upper = products.astype(jnp.bfloat16)
            lower = (products - upper.astype(jnp.float32)).astype(jnp.bfloat16)
            ones = jnp.ones((8, head_size), jnp.bfloat16)
            stats_out[1][part] = dot_nt(ones, upper) + dot_nt(ones, lower)
            write_rows(part, attended)
        return 0

    def write_rows(part, rows):
        for number in range(2):

            @pl.when(part == number)
            def _():
                rows_out[number][...] = rows

    def backward_part(part, _):
        facts = part_facts(part)
        log_total, out_dot = stats[0][part][:1], stats[1][part][:1]
        dq_new = dq_out[0]
        dq_new[part] = jnp.zeros((head_size, lanes), jnp.float32) if finish else dq_in[0][part]

        def differentiate(unit, rows, masked):
            probs = jnp.exp2(scores_of(unit, rows, part, facts, masked) * log2_scale - log_total)
            dprobs = dot_nt(v_scr[unit, rows, :], g_scr[part])
            dscores = (probs * (dprobs - out_dot)).astype(jnp.bfloat16)
            dv_scr[unit, rows, :] += dot_nn(probs.astype(jnp.bfloat16), g_scr[part])
            dk_scr[unit, rows, :] += dot_nn(dscores, q_scr[part])
            dq_new[part] += dot_tn(k_scr[unit, rows, :], dscores)

        each_unit(facts, differentiate)
        if last:
            write_rows(part, (dq_new[part] * scale).T.astype(jnp.bfloat16))
        return 0

    if forward:
        lax.fori_loop(0, 2, forward_part, 0)
    if backward:
        dk_scr[...] = jnp.zeros_like(dk_scr)
        dv_scr[...] = jnp.zeros_like(dv_scr)
        lax.fori_loop(0, 2, backward_part, 0)
        for unit, half, piece, slot in places():
            rows = pl.ds(half * block, block)
            grads[piece][slot, 0] = (dk_scr[unit, rows, :] * scale).astype(jnp.bfloat16)
            grads[piece][slot, 1] = dv_scr[unit, rows, :].astype(jnp.bfloat16)


def run_stage(step, phases, block, group, docs, spot, q_parts, g_parts, pieces, state=(), stats=(), dq=(), after=(), passing=()):
    forward, finish, backward, last = phases
    kind = {0: "own", 4: "far"}.get(step, "pair")
    stage = (kind, *phases)
    units = 4 if kind == "pair" else 2
    y, z = spot
    place = jnp.stack([y, z, jnp.where(z % 2 == 0, step, -step)]).astype(jnp.int32)
    lanes, head_size = q_parts[0].shape
    f32 = lambda *shape: jax.ShapeDtypeStruct(shape, jnp.float32)
    low = lambda array: jax.ShapeDtypeStruct(array.shape, jnp.bfloat16)
    state_shapes = [f32(2, 8, lanes), f32(2, 8, lanes), f32(2, head_size, lanes)]
    dq_shape = f32(2, head_size, lanes)
    operands = [*after, docs, place, *q_parts, *(g_parts if backward else ()), *pieces, *state, *stats, *dq, *passing]
    outs = []
    aliases = {}
    if forward and not finish:
        if state:
            aliases = {len(operands) - 3 + n: n for n in range(3)}
        outs += state_shapes
    if finish or last:
        outs += [low(q) for q in q_parts]
    if finish:
        outs += state_shapes[:2]
    if backward and not last:
        if dq:
            aliases = {len(operands) - 1: len(outs)}
        outs += [dq_shape]
    if backward:
        outs += [low(piece) for piece in pieces]
    for number, array in enumerate(passing):
        aliases[len(operands) - len(passing) + number] = len(outs)
        outs += [low(array)]
    scratch = [
        pltpu.VMEM((units, 2 * block, head_size), jnp.bfloat16),
        pltpu.VMEM((units, 2 * block, head_size), jnp.bfloat16),
        pltpu.VMEM((2, lanes, head_size), jnp.bfloat16),
    ]
    if finish:
        scratch += [pltpu.VMEM(shape.shape, jnp.float32) for shape in state_shapes]
    if backward:
        scratch += [
            pltpu.VMEM((2, lanes, head_size), jnp.bfloat16),
            pltpu.VMEM((units, 2 * block, head_size), jnp.float32),
            pltpu.VMEM((units, 2 * block, head_size), jnp.float32),
        ]
    if last:
        scratch += [pltpu.VMEM(dq_shape.shape, jnp.float32)]
    smem = pl.BlockSpec(memory_space=pltpu.SMEM)
    vmem = pl.BlockSpec(memory_space=pltpu.VMEM)
    anywhere = pl.BlockSpec(memory_space=pl.ANY)
    inside = len(operands) - 2 - len(after) - len(passing)
    products = 2 * forward + 5 * backward
    return pl.pallas_call(
        functools.partial(stage_kernel, stage, len(after), len(passing), block, group),
        out_shape=outs,
        in_specs=[anywhere] * len(after) + [smem, smem] + [vmem] * inside + [anywhere] * len(passing),
        out_specs=[vmem] * (len(outs) - len(passing)) + [anywhere] * len(passing),
        scratch_shapes=scratch,
        input_output_aliases=aliases,
        compiler_params=pltpu.CompilerParams(vmem_limit_bytes=24 * 1024 * 1024),
        cost_estimate=pl.CostEstimate(
            flops=6 * products * 2 * lanes * units * 2 * block * head_size,
            bytes_accessed=4 * 1024 * 1024,
            transcendentals=2 * lanes * units * 2 * block,
        ),
        name="fwd" * forward + "bwd" * backward + kind,
    )(*operands)


def swap_y(mask):
    return [(y * NZ + z, (y ^ mask) * NZ + z) for y in range(NY) for z in range(NZ)]


def swap_z(first):
    turns = [1 if z % 2 == first else -1 for z in range(NZ)]
    return [(y * NZ + z, y * NZ + (z + turns[z]) % NZ) for y in range(NY) for z in range(NZ)]


MIRROR = swap_y(NY - 1)


def add_up(one, other):
    return (one.astype(jnp.float32) + other.astype(jnp.float32)).astype(jnp.bfloat16)


def swap_even(array):
    return lax.ppermute(array, "ctx", swap_z(0))


def swap_odd(array):
    return lax.ppermute(array, "ctx", swap_z(1))


def on_device(queries, key_rows, values, out_grad, doc_lengths):
    block, query_heads, head_size = queries.shape
    key_heads = key_rows.shape[1]
    group = query_heads // key_heads
    place = lax.axis_index("ctx")
    y, z = place // NZ, place % NZ
    mine = y // 2

    def head_of(array, number, width):
        picked = jnp.where(number == 0, array[:, :width], array[:, width:])
        return picked.reshape(block * width, head_size)

    def key_pair(number):
        return jnp.stack([head_of(key_rows, number, 1), head_of(values, number, 1)])

    pairs = [key_pair(mine), key_pair(1 - mine)]
    held = [lax.ppermute(pairs[mask // 2], "ctx", swap_y(mask)) for mask in (1, 3, 2)]
    column = jnp.stack([pairs[0], *held])

    q_parts = [head_of(queries, mine, group), lax.ppermute(head_of(queries, 1 - mine, group), "ctx", MIRROR)]
    g_own, g_leaving = head_of(out_grad, mine, group), head_of(out_grad, 1 - mine, group)
    run = functools.partial(
        run_stage, block=block, group=group, docs=doc_lengths, spot=(y, z), q_parts=q_parts
    )

    evens, odds = [column], [column]
    state = ()
    for step in range(4):
        pieces = [column] if step == 0 else [evens[step], odds[step]]
        if step < 3:
            even, odd = swap_even(odds[step]), swap_odd(evens[step])
        else:
            even, odd = swap_even(odds[step][:2]), swap_odd(evens[step][2:])
        evens.append(even)
        odds.append(odd)
        passing = () if step else (g_leaving,)
        state = run(step, (True, False, False, False), g_parts=(), pieces=pieces, state=state, passing=passing)
        if passing:
            g_parts = [g_own, lax.ppermute(state[3], "ctx", MIRROR)]
            state = state[:3]
    run = functools.partial(run, g_parts=g_parts)
    own_out, other_out, log_total, out_dot, dq, even_grad, odd_grad = run(
        4, (True, True, True, False), pieces=[evens[4], odds[4]], state=state
    )
    stats = (log_total, out_dot)
    other_out = lax.ppermute(other_out, "ctx", MIRROR)
    even, odd = swap_even(even_grad), swap_odd(odd_grad)
    after = ()
    for step in (3, 2, 1):
        dq, even_grad, odd_grad = run(
            step, (False, False, True, False), pieces=[evens[step], odds[step]], stats=stats, dq=(dq,), after=after
        )
        if step == 3:
            odd_grad = jnp.concatenate([add_up(odd_grad[:2], even), odd_grad[2:]], axis=0)
            even_grad = jnp.concatenate([even_grad[:2], add_up(even_grad[2:], odd)], axis=0)
        else:
            odd_grad, even_grad = add_up(odd_grad, even), add_up(even_grad, odd)
        after = (even_grad, odd_grad)
        even, odd = swap_even(even_grad), swap_odd(odd_grad)
    own_dq, other_dq, grad, other_out = run(
        0, (False, False, True, True), pieces=[column], stats=stats, dq=(dq,), after=after, passing=(other_out,)
    )
    other_dq = lax.ppermute(other_dq, "ctx", MIRROR)
    sums = grad.astype(jnp.float32) + even.astype(jnp.float32) + odd.astype(jnp.float32)

    def both_heads(own, other):
        one, two = (r.reshape(block, group, head_size) for r in (own, other))
        return jnp.concatenate([jnp.where(mine == 0, one, two), jnp.where(mine == 0, two, one)], axis=1)

    attended, query_grad = both_heads(own_out, other_out), both_heads(own_dq, other_dq)
    arrived = {
        mask: lax.ppermute(sums[slot].astype(jnp.bfloat16), "ctx", swap_y(mask)).astype(jnp.float32)
        for slot, mask in ((3, 2), (2, 3), (1, 1))
    }
    far, near = arrived[2] + arrived[3], arrived[1] + sums[0]
    heads = [jnp.where(mine == 1, far, near), jnp.where(mine == 1, near, far)]
    grads = jnp.stack(heads, axis=2).astype(jnp.bfloat16)
    return attended, query_grad, grads[0], grads[1]


def solution(mesh):
    placed = (
        P(("dp", "ctx"), "head", None),
        P(("dp", "ctx"), "head", None),
        P(("dp", "ctx"), "head", None),
        P(("dp", "ctx"), "head", None),
        P("dp"),
    )
    return jax.shard_map(
        on_device,
        mesh=mesh,
        in_specs=placed,
        out_specs=(
            P(("dp", "ctx"), "head", None),
            P(("dp", "ctx"), "head", None),
            P(("dp", "ctx"), "head", None),
            P(("dp", "ctx"), "head", None),
        ),
        check_vma=False,
    )
```
